32 devices in a mesh: tm: 4 (over x, core), mic: 8 (over z, y).
Axes of the slice: x: 2, y: 2, z: 4, core: 2. Of those that a mesh axis runs over, the one named last changes fastest.
Arguments:
- samples: bfloat16 [32, 4096, 4096], P('tm', 'mic'), may hold values from -6 to 6
- bin_ids: int32 [16], replicated, may hold values from 1 to 2047
- delays: int32 [1024, 4096], P('mic'), may hold values from 0 to 1023
Outputs:
- source_map: float32 [16, 1024], P('tm', 'mic')
The draws below stay inside these ranges and needn't reach their ends.
All inputs are finite; a program needn't handle non-finite values.
Results may differ from the reference program's by a relative error of at most 0.0013.
Values may be sent and summed in bfloat16 or wider, within the bound.
A program may use at most 64 MiB of HBM per device.

```python
import math
import jax
import jax.numpy as jnp
from jax import lax

MICS = 4096
L = 4096
F = 16
SEGS = 32
POINTS = 1024


def with_ends(entries, own_key, smallest, largest):
    longest = entries.shape.index(max(entries.shape))
    spots = []
    for shift in (0, 1):
        where = [jax.random.randint(jax.random.fold_in(own_key, axis), (), 0, length) for axis, length in enumerate(entries.shape)]
        where[longest] = (where[longest] + shift) % entries.shape[longest]
        spots.append(tuple(where))
    return entries.at[spots[0]].set(smallest).at[spots[1]].set(largest)


def shard_levels(rng, dims, split, least, top_value):
    def one(position, blocks):
        draws = jax.random.uniform(jax.random.fold_in(jax.random.fold_in(rng, 6), position), (blocks,), jnp.float32, least / len(split), top_value / len(split))
        return jnp.repeat(jnp.exp(draws), dims[position] // blocks).reshape((-1,) + (1,) * (len(dims) - position - 1))

    level = one(*split[0])
    for cut in split[1:]:
        level = level * one(*cut)
    return level


def gaussian(key, dims, scale, limit, split=(), kind=jnp.bfloat16):
    factor_of = shard_levels(key, dims, split, -0.22, 0.18) if split else 1.0
    drawn = jax.random.normal(key, dims, jnp.float32) * scale * factor_of
    return jnp.minimum(jnp.maximum(drawn, -limit), limit).astype(kind)


def setup_inputs(seed: int = 0) -> dict:
    key_list = jax.random.split(jax.random.key(seed), 4)
    samples = gaussian(key_list[0], (SEGS, MICS, L), 1.0, 6.0, ((0, 4), (1, 8)))
    bin_ids = with_ends(jax.random.randint(key_list[1], (F,), 1, L // 2), jax.random.fold_in(key_list[1], 1), 1, (L // 2) - 1).astype(jnp.int32)
    delays = with_ends(jax.random.randint(key_list[2], (POINTS, MICS), 0, 1024), jax.random.fold_in(key_list[2], 1), 0, 1023).astype(jnp.int32)
    return dict(samples=samples, bin_ids=bin_ids, delays=delays)


def dft_table(bin_ids, length):
    sample_index = jnp.arange(length, dtype=jnp.int32)
    window = 0.5 - 0.5 * jnp.cos(2.0 * jnp.pi * sample_index.astype(jnp.float32) / length)
    window_norm = jnp.sqrt(jnp.sum(window * window))
    phase_index = sample_index[:, None] * bin_ids[None, :] % length
    angles = 2.0 * jnp.pi * phase_index.astype(jnp.float32) / length
    cosine = window[:, None] * jnp.cos(angles) / window_norm
    sine_part = -window[:, None] * jnp.sin(angles) / window_norm
    return jnp.stack([cosine, sine_part], axis=-1).reshape(length, -1).astype(jnp.bfloat16)

def reference(samples, bin_ids, delays):
    transform_rows = dft_table(bin_ids, L).astype(jnp.float32)

    def transform(segment):
        result = jnp.dot(segment.astype(jnp.float32), transform_rows, precision=lax.Precision.HIGHEST)
        return result.T.reshape(F, 2, MICS).astype(jnp.bfloat16)
    spectra = lax.map(transform, samples)

    def per_bin(entry):
        bin_value, values = entry
        phases = 2.0 * jnp.pi * (bin_value * delays % L).astype(jnp.float32) / L
        cos_part = jnp.cos(phases).astype(jnp.bfloat16).astype(jnp.float32)
        sin_part = jnp.sin(phases).astype(jnp.bfloat16).astype(jnp.float32)
        flat = values.reshape(SEGS * 2, MICS).astype(jnp.float32)
        along_cos = jnp.dot(flat, cos_part.T, precision=lax.Precision.HIGHEST).reshape(SEGS, 2, POINTS)
        along_sin = jnp.dot(flat, sin_part.T, precision=lax.Precision.HIGHEST).reshape(SEGS, 2, POINTS)
        real_part = (along_cos[:, 0] - along_sin[:, 1]) / math.sqrt(MICS)
        imag_part = (along_cos[:, 1] + along_sin[:, 0]) / math.sqrt(MICS)
        return lax.optimization_barrier(jnp.sum(real_part * real_part + imag_part * imag_part, axis=0)) / SEGS
    return lax.map(per_bin, (bin_ids, jnp.moveaxis(spectra, 1, 0)))
```

```python
import functools
import math

import jax
import jax.numpy as jnp
import numpy as np
from jax import lax
from jax.experimental import pallas as pl
from jax.experimental.pallas import tpu as pltpu
from jax.sharding import PartitionSpec as P

MESH = pl.DeviceIdType.MESH
NT = (((1,), (1,)), ((), ()))


def fit(function, count):
    nodes = 0.125 + 0.125 * np.cos(np.pi * (np.arange(64) + 0.5) / 64)
    series = np.polynomial.chebyshev.Chebyshev.fit(nodes, function(np.sqrt(nodes)), count - 1, domain=[0, 0.25])
    return [float(c) for c in series.convert(kind=np.polynomial.Polynomial).coef]


SIN_HALF = fit(lambda r: np.sin(np.pi * r) / r, 5)
COS_HALF = fit(lambda r: np.cos(np.pi * r), 6)


def horner(coefficients, y):
    total = coefficients[-1]
    for c in coefficients[-2::-1]:
        total = total * y + c
    return total


def fraction(turns):
    return turns - ((turns + 12582912.0) - 12582912.0)


def cos_turns(turns):
    r = fraction(turns)
    s = r * horner(SIN_HALF, r * r)
    return 1.0 - (s + s) * s


def cos_sin_turns(turns):
    r = fraction(turns)
    y = r * r
    s = r * horner(SIN_HALF, y)
    twice = s + s
    return 1.0 - twice * s, twice * horner(COS_HALF, y)


def kernel(dims, bins, samples, delays, out, table, held, delay, spec, gath, steer, acc,
           sample_sem, delay_sem, send_sem, fwd_sem, recv_sem):
    T, Z, Y, bin_count, nb, chunk_segs, chunks, parts, group, slots = dims
    mics_here, length = samples.shape[1], samples.shape[2]
    points, mics = delays.shape
    rows = chunk_segs * 2 * nb
    steps = chunks * parts
    t, m = lax.axis_index("tm"), lax.axis_index("mic")
    z, y = lax.div(m, Y), lax.rem(m, Y)

    def mic_of(z2, y2):
        return z2 * Y + y2

    def fetch(i, slot):
        c, q = lax.div(i, parts), lax.rem(i, parts)
        return pltpu.make_async_copy(
            samples.at[pl.ds(c * chunk_segs, chunk_segs), pl.ds(pl.multiple_of(q * group, group), group)],
            held.at[slot], sample_sem.at[slot])

    for i in range(min(slots, steps)):
        fetch(i, i).start()
        if i == 0:
            pltpu.make_async_copy(delays, delay, delay_sem).start()

    near = [(lax.rem(t + a, T), mic_of(lax.rem(z + k, Z), y)) for k in range(Z) for a in range(T) if k or a]
    across = [(lax.rem(t + a, T), mic_of(z, 1 - y)) for a in range(T)] if Y == 2 else []
    peers = near + across
    barrier = pltpu.get_barrier_semaphore()
    for t2, m2 in peers:
        pl.semaphore_signal(barrier, inc=1, device_id={"tm": t2, "mic": m2}, device_id_type=MESH)

    table_rows = 2 * bin_count
    row = lax.broadcasted_iota(jnp.int32, (table_rows, 128), 0)
    lane = lax.broadcasted_iota(jnp.int32, (table_rows, 128), 1)
    bin_of = (row // (2 * nb)) * nb + row % nb
    scale = jnp.zeros((table_rows, 128), jnp.float32)
    for i in range(bin_count):
        scale = jnp.where(bin_of == i, bins[i].astype(jnp.float32) * (1.0 / length), scale)
    quarter = jnp.where((row // nb) % 2 == 1, jnp.float32(0.25), jnp.float32(0.0))
    lane8 = lax.broadcasted_iota(jnp.int32, (8, 128), 1)

    def window_at(j, like):
        return 0.5 - 0.5 * cos_turns((like + j * 128).astype(jnp.float32) * (1.0 / length))

    def norm_step(j, total):
        w = window_at(j, lane8)
        return total + w * w

    norm = jnp.sum(lax.fori_loop(0, length // 128, norm_step, jnp.zeros((8, 128), jnp.float32), unroll=4),
                   axis=1, keepdims=True)[0:1]
    inverse = 1.0 / jnp.sqrt(norm)

    def table_step(j, carry):
        w = window_at(j, lane8)[0:1] * inverse
        turns = (lane + j * 128).astype(jnp.float32) * scale + quarter
        table[:, pl.ds(pl.multiple_of(j * 128, 128), 128)] = (w * cos_turns(turns)).astype(jnp.bfloat16)
        return carry

    lax.fori_loop(0, length // 128, table_step, 0, unroll=4)

    pltpu.make_async_copy(delays, delay, delay_sem).wait()
    own_scale = [bins[t * nb + b].astype(jnp.float32) * (1.0 / length) for b in range(nb)]
    point_part = points // steps
    width = 512 if mics % 512 == 0 else 128

    def block_rows(c):
        return pl.ds(pl.multiple_of(c * T * rows, T * rows), T * rows)

    def push(c, index, t2, m2):
        return pltpu.make_async_remote_copy(
            src_ref=spec.at[c, pl.ds(pl.multiple_of(t2 * rows, rows), rows)],
            dst_ref=gath.at[m, pl.ds(pl.multiple_of(c * T * rows + t * rows, rows), rows)],
            send_sem=send_sem.at[c, index], recv_sem=recv_sem.at[c, m],
            device_id={"tm": t2, "mic": m2}, device_id_type=MESH)

    def forward(c, k):
        m2 = mic_of(lax.rem(z + k, Z), y)
        return pltpu.make_async_remote_copy(
            src_ref=gath.at[m2, block_rows(c)], dst_ref=gath.at[m2, block_rows(c)],
            send_sem=fwd_sem.at[c, k - 1], recv_sem=recv_sem.at[c, m2],
            device_id={"tm": t, "mic": mic_of(z, 1 - y)}, device_id_type=MESH)

    def arrived(c, m2):
        pltpu.make_async_copy(gath.at[m2, block_rows(c)], gath.at[m2, block_rows(c)], recv_sem.at[c, m2]).wait()

    def send_chunk(c):
        for index, (t2, m2) in enumerate(peers):
            push(c, index, t2, m2).start()
        pltpu.make_async_copy(
            spec.at[c, pl.ds(pl.multiple_of(t * rows, rows), rows)],
            gath.at[m, pl.ds(pl.multiple_of(c * T * rows + t * rows, rows), rows)],
            recv_sem.at[c, m]).start()

    def pass_on(c):
        for k in range(1, Z):
            arrived(c, mic_of(lax.rem(z + k, Z), y))
            if Y == 2:
                forward(c, k).start()

    pl.semaphore_wait(barrier, len(peers))

    def step(i, carry):
        slot = lax.rem(i, slots)
        c, q = lax.div(i, parts), lax.rem(i, parts)
        fetch(i, slot).wait()
        block = held[slot].reshape(chunk_segs * group, length)
        found = lax.dot_general(block, table[...], NT, preferred_element_type=jnp.float32)
        first = pl.multiple_of(i * point_part, point_part)
        for start in range(0, mics, width):
            turns = delay[pl.ds(first, point_part), start:start + width].astype(jnp.float32)
            for b in range(nb):
                cosine, sine = cos_sin_turns(turns * own_scale[b])
                steer[b, 0, pl.ds(first, point_part), start:start + width] = cosine.astype(jnp.bfloat16)
                steer[b, 1, pl.ds(first, point_part), start:start + width] = sine.astype(jnp.bfloat16)
        found = [found[s * group:(s + 1) * group].T for s in range(chunk_segs)]
        for t2 in range(T):
            lines = [f[t2 * 2 * nb:(t2 + 1) * 2 * nb] for f in found]
            spec[c, t2 * rows:(t2 + 1) * rows, pl.ds(pl.multiple_of(q * group, group), group)] = (
                jnp.concatenate(lines, axis=0).astype(jnp.bfloat16))

        @pl.when(i + slots < steps)
        def _():
            fetch(i + slots, slot).start()

        @pl.when(q == parts - 1)
        def _():
            send_chunk(c)

            @pl.when(c >= 1)
            def _():
                pass_on(c - 1)

        return carry

    lax.fori_loop(0, steps, step, 0)
    pass_on(chunks - 1)

    acc[...] = jnp.zeros_like(acc)

    def add_block(m2):
        columns = pl.ds(pl.multiple_of(m2 * mics_here, mics_here), mics_here)
        lhs = steer[:, :, :, columns].reshape(nb * 2 * points, mics_here)
        acc[...] += lax.dot_general(lhs, gath[m2], NT, preferred_element_type=jnp.float32)

    def own_y(k, carry):
        m2 = mic_of(lax.rem(z + k, Z), y)

        @pl.when(k == 0)
        def _():
            for c in range(chunks):
                arrived(c, m2)

        add_block(m2)
        return carry

    lax.fori_loop(0, Z, own_y, 0)

    def other_y(k, carry):
        m2 = mic_of(lax.rem(z + k, Z), 1 - y)
        for c in range(chunks):
            arrived(c, m2)
        add_block(m2)
        return carry

    if Y == 2:
        lax.fori_loop(0, Z, other_y, 0)

    columns = chunks * T * rows
    column = lax.broadcasted_iota(jnp.int32, (points, columns), 1)
    for b in range(nb):
        along_cos = acc[(2 * b) * points:(2 * b + 1) * points]
        along_sin = acc[(2 * b + 1) * points:(2 * b + 2) * points]
        real = along_cos - pltpu.roll(along_sin, columns - nb, axis=1)
        imag = pltpu.roll(along_cos, columns - nb, axis=1) + along_sin
        power = jnp.where(column % (2 * nb) == b, real * real + imag * imag, 0.0)
        out[b:b + 1, :] = jnp.sum(power.T, axis=0, keepdims=True) * (
            1.0 / (mics * chunks * chunk_segs * T))

    def drain(c, carry):
        for index, (t2, m2) in enumerate(peers):
            push(c, index, t2, m2).wait_send()
        if Y == 2:
            for k in range(1, Z):
                forward(c, k).wait_send()
        return carry

    lax.fori_loop(0, chunks, drain, 0)


def per_device(T, M, samples, bin_ids, delays):
    segs, mics_here, length = samples.shape
    points, mics = delays.shape
    bin_count = bin_ids.shape[0]
    Y = 2 if M % 2 == 0 else 1
    Z = M // Y
    nb = bin_count // T
    chunk_segs = max(1, 16 // (2 * nb))
    chunks = segs // chunk_segs
    group = min(mics_here, 256)
    parts = mics_here // group
    slots = 4
    rows = chunk_segs * 2 * nb
    peers = T * Z - 1 + (T if Y == 2 else 0)
    dims = (T, Z, Y, bin_count, nb, chunk_segs, chunks, parts, group, slots)
    DMA = pltpu.SemaphoreType.DMA
    return pl.pallas_call(
        functools.partial(kernel, dims),
        out_shape=jax.ShapeDtypeStruct((nb, points), jnp.float32),
        in_specs=[
            pl.BlockSpec(memory_space=pltpu.SMEM),
            pl.BlockSpec(memory_space=pl.ANY),
            pl.BlockSpec(memory_space=pl.ANY),
        ],
        out_specs=pl.BlockSpec(memory_space=pltpu.VMEM),
        scratch_shapes=[
            pltpu.VMEM((2 * bin_count, length), jnp.bfloat16),
            pltpu.VMEM((slots, chunk_segs, group, length), jnp.bfloat16),
            pltpu.VMEM((points, mics), jnp.int32),
            pltpu.VMEM((chunks, T * rows, mics_here), jnp.bfloat16),
            pltpu.VMEM((M, chunks * T * rows, mics_here), jnp.bfloat16),
            pltpu.VMEM((nb, 2, points, mics), jnp.bfloat16),
            pltpu.VMEM((nb * 2 * points, chunks * T * rows), jnp.float32),
            DMA((slots,)),
            DMA(()),
            DMA((chunks, peers)),
            DMA((chunks, max(Z - 1, 1))),
            DMA((chunks, M)),
        ],
        compiler_params=pltpu.CompilerParams(
            collective_id=0, has_side_effects=True, vmem_limit_bytes=56 * 1024 * 1024),
        cost_estimate=pl.CostEstimate(
            flops=2 * samples.size * 2 * bin_count, bytes_accessed=samples.size * 2, transcendentals=0),
    )(bin_ids, samples, delays)


def solution(mesh):
    placed = (P("tm", "mic", None), P(), P("mic", None))
    return jax.shard_map(
        functools.partial(per_device, mesh.shape["tm"], mesh.shape["mic"]),
        mesh=mesh, in_specs=placed, out_specs=P("tm", "mic"), check_vma=False)
```

```python
import functools
import math

import jax
import jax.numpy as jnp
import numpy as np
from jax import lax
from jax.experimental import pallas as pl
from jax.experimental.pallas import tpu as pltpu
from jax.sharding import PartitionSpec as P

MESH = pl.DeviceIdType.MESH
NT = (((1,), (1,)), ((), ()))


def fit(function, count):
    nodes = 0.125 + 0.125 * np.cos(np.pi * (np.arange(64) + 0.5) / 64)
    series = np.polynomial.chebyshev.Chebyshev.fit(nodes, function(np.sqrt(nodes)), count - 1, domain=[0, 0.25])
    return [float(c) for c in series.convert(kind=np.polynomial.Polynomial).coef]


SIN_HALF = fit(lambda r: np.sin(np.pi * r) / r, 5)
COS_HALF = fit(lambda r: np.cos(np.pi * r), 6)


def horner(coefficients, y):
    total = coefficients[-1]
    for c in coefficients[-2::-1]:
        total = total * y + c
    return total


def fraction(turns):
    return turns - ((turns + 12582912.0) - 12582912.0)


def cos_turns(turns):
    r = fraction(turns)
    s = r * horner(SIN_HALF, r * r)
    return 1.0 - (s + s) * s


def cos_sin_turns(turns):
    r = fraction(turns)
    y = r * r
    s = r * horner(SIN_HALF, y)
    twice = s + s
    return 1.0 - twice * s, twice * horner(COS_HALF, y)


def kernel(dims, bins, samples, delays, out, table, held, delay, spec, gath, steer, acc,
           sample_sem, delay_sem, send_sem, fwd_sem, recv_sem):
    T, Z, Y, bin_count, nb, chunk_segs, chunks, parts, group, slots = dims
    mics_here, length = samples.shape[1], samples.shape[2]
    points, mics = delays.shape
    rows = chunk_segs * 2 * nb
    steps = chunks * parts
    t, m = lax.axis_index("tm"), lax.axis_index("mic")
    z, y = lax.div(m, Y), lax.rem(m, Y)

    def mic_of(z2, y2):
        return z2 * Y + y2

    def fetch(i, slot):
        c, q = lax.div(i, parts), lax.rem(i, parts)
        return pltpu.make_async_copy(
            samples.at[pl.ds(c * chunk_segs, chunk_segs), pl.ds(pl.multiple_of(q * group, group), group)],
            held.at[slot], sample_sem.at[slot])

    for i in range(min(slots, steps)):
        fetch(i, i).start()
        if i == 0:
            pltpu.make_async_copy(delays, delay, delay_sem).start()

    near = [(lax.rem(t + a, T), mic_of(lax.rem(z + k, Z), y)) for k in range(Z) for a in range(T) if k or a]
    across = [(lax.rem(t + a, T), mic_of(z, 1 - y)) for a in range(T)] if Y == 2 else []
    peers = near + across
    barrier = pltpu.get_barrier_semaphore()
    for t2, m2 in peers:
        pl.semaphore_signal(barrier, inc=1, device_id={"tm": t2, "mic": m2}, device_id_type=MESH)

    table_rows = 2 * bin_count
    row = lax.broadcasted_iota(jnp.int32, (table_rows, 128), 0)
    lane = lax.broadcasted_iota(jnp.int32, (table_rows, 128), 1)
    bin_of = (row // (2 * nb)) * nb + row % nb
    scale = jnp.zeros((table_rows, 128), jnp.float32)
    for i in range(bin_count):
        scale = jnp.where(bin_of == i, bins[i].astype(jnp.float32) * (1.0 / length), scale)
    quarter = jnp.where((row // nb) % 2 == 1, jnp.float32(0.25), jnp.float32(0.0))
    lane8 = lax.broadcasted_iota(jnp.int32, (8, 128), 1)

    def window_at(j, like):
        return 0.5 - 0.5 * cos_turns((like + j * 128).astype(jnp.float32) * (1.0 / length))

    def norm_step(j, total):
        w = window_at(j, lane8)
        return total + w * w

    norm = jnp.sum(lax.fori_loop(0, length // 128, norm_step, jnp.zeros((8, 128), jnp.float32), unroll=4),
                   axis=1, keepdims=True)[0:1]
    inverse = 1.0 / jnp.sqrt(norm)

    def table_step(j, carry):
        w = window_at(j, lane8)[0:1] * inverse
        turns = (lane + j * 128).astype(jnp.float32) * scale + quarter
        table[:, pl.ds(pl.multiple_of(j * 128, 128), 128)] = (w * cos_turns(turns)).astype(jnp.bfloat16)
        return carry

    lax.fori_loop(0, length // 128, table_step, 0, unroll=4)

    own_scale = [bins[t * nb + b].astype(jnp.float32) * (1.0 / length) for b in range(nb)]
    point_part = points // steps
    width = 512 if mics % 512 == 0 else 128

    def block_rows(c):
        return pl.ds(pl.multiple_of(c * T * rows, T * rows), T * rows)

    def push(c, index, t2, m2):
        return pltpu.make_async_remote_copy(
            src_ref=spec.at[c, pl.ds(pl.multiple_of(t2 * rows, rows), rows)],
            dst_ref=gath.at[m, pl.ds(pl.multiple_of(c * T * rows + t * rows, rows), rows)],
            send_sem=send_sem.at[c, index], recv_sem=recv_sem.at[c, m],
            device_id={"tm": t2, "mic": m2}, device_id_type=MESH)

    def forward(c, k):
        m2 = mic_of(lax.rem(z + k, Z), y)
        return pltpu.make_async_remote_copy(
            src_ref=gath.at[m2, block_rows(c)], dst_ref=gath.at[m2, block_rows(c)],
            send_sem=fwd_sem.at[c, k - 1], recv_sem=recv_sem.at[c, m2],
            device_id={"tm": t, "mic": mic_of(z, 1 - y)}, device_id_type=MESH)

    def arrived(c, m2):
        pltpu.make_async_copy(gath.at[m2, block_rows(c)], gath.at[m2, block_rows(c)], recv_sem.at[c, m2]).wait()

    def send_chunk(c):
        for index, (t2, m2) in enumerate(peers):
            push(c, index, t2, m2).start()
        pltpu.make_async_copy(
            spec.at[c, pl.ds(pl.multiple_of(t * rows, rows), rows)],
            gath.at[m, pl.ds(pl.multiple_of(c * T * rows + t * rows, rows), rows)],
            recv_sem.at[c, m]).start()

    def pass_on(c):
        for k in range(1, Z):
            arrived(c, mic_of(lax.rem(z + k, Z), y))
            if Y == 2:
                forward(c, k).start()

    pl.semaphore_wait(barrier, len(peers))

    def step(i, carry):
        slot = lax.rem(i, slots)
        c, q = lax.div(i, parts), lax.rem(i, parts)
        fetch(i, slot).wait()
        block = held[slot].reshape(chunk_segs * group, length)
        found = lax.dot_general(block, table[...], NT, preferred_element_type=jnp.float32)
        found = [found[s * group:(s + 1) * group].T for s in range(chunk_segs)]
        for t2 in range(T):
            lines = [f[t2 * 2 * nb:(t2 + 1) * 2 * nb] for f in found]
            spec[c, t2 * rows:(t2 + 1) * rows, pl.ds(pl.multiple_of(q * group, group), group)] = (
                jnp.concatenate(lines, axis=0).astype(jnp.bfloat16))

        @pl.when(i + slots < steps)
        def _():
            fetch(i + slots, slot).start()

        @pl.when(q == parts - 1)
        def _():
            send_chunk(c)

            @pl.when(c >= 2)
            def _():
                @pl.when(c < chunks - 1)
                def _():
                    pass_on(c - 2)

        return carry

    lax.fori_loop(0, steps, step, 0)

    pltpu.make_async_copy(delays, delay, delay_sem).wait()
    late = list(range(max(0, chunks - 3), chunks))
    turn_of = {(n * steps) // len(late) + 1: c for n, c in enumerate(late[:-1])}

    def steer_step(i, carry):
        first = pl.multiple_of(i * point_part, point_part)
        for start in range(0, mics, width):
            turns = delay[pl.ds(first, point_part), start:start + width].astype(jnp.float32)
            for b in range(nb):
                cosine, sine = cos_sin_turns(turns * own_scale[b])
                steer[b, 0, pl.ds(first, point_part), start:start + width] = cosine.astype(jnp.bfloat16)
                steer[b, 1, pl.ds(first, point_part), start:start + width] = sine.astype(jnp.bfloat16)
        for turn, c in turn_of.items():
            @pl.when(i == turn)
            def _():
                pass_on(c)

        return carry

    lax.fori_loop(0, steps, steer_step, 0)
    pass_on(late[-1])

    acc[...] = jnp.zeros_like(acc)

    def add_block(m2):
        columns = pl.ds(pl.multiple_of(m2 * mics_here, mics_here), mics_here)
        lhs = steer[:, :, :, columns].reshape(nb * 2 * points, mics_here)
        acc[...] += lax.dot_general(lhs, gath[m2], NT, preferred_element_type=jnp.float32)

    def own_y(k, carry):
        m2 = mic_of(lax.rem(z + k, Z), y)

        @pl.when(k == 0)
        def _():
            for c in range(chunks):
                arrived(c, m2)

        add_block(m2)
        return carry

    lax.fori_loop(0, Z, own_y, 0)

    def other_y(k, carry):
        m2 = mic_of(lax.rem(z + k, Z), 1 - y)
        for c in range(chunks):
            arrived(c, m2)
        add_block(m2)
        return carry

    if Y == 2:
        lax.fori_loop(0, Z, other_y, 0)

    columns = chunks * T * rows
    column = lax.broadcasted_iota(jnp.int32, (points, columns), 1)
    for b in range(nb):
        along_cos = acc[(2 * b) * points:(2 * b + 1) * points]
        along_sin = acc[(2 * b + 1) * points:(2 * b + 2) * points]
        real = along_cos - pltpu.roll(along_sin, columns - nb, axis=1)
        imag = pltpu.roll(along_cos, columns - nb, axis=1) + along_sin
        power = jnp.where(column % (2 * nb) == b, real * real + imag * imag, 0.0)
        out[b:b + 1, :] = jnp.sum(power.T, axis=0, keepdims=True) * (
            1.0 / (mics * chunks * chunk_segs * T))

    def drain(c, carry):
        for index, (t2, m2) in enumerate(peers):
            push(c, index, t2, m2).wait_send()
        if Y == 2:
            for k in range(1, Z):
                forward(c, k).wait_send()
        return carry

    lax.fori_loop(0, chunks, drain, 0)


def per_device(T, M, samples, bin_ids, delays):
    segs, mics_here, length = samples.shape
    points, mics = delays.shape
    bin_count = bin_ids.shape[0]
    Y = 2 if M % 2 == 0 else 1
    Z = M // Y
    nb = bin_count // T
    chunk_segs = max(1, 16 // (2 * nb))
    chunks = segs // chunk_segs
    group = min(mics_here, 256)
    parts = mics_here // group
    slots = 4
    rows = chunk_segs * 2 * nb
    peers = T * Z - 1 + (T if Y == 2 else 0)
    dims = (T, Z, Y, bin_count, nb, chunk_segs, chunks, parts, group, slots)
    DMA = pltpu.SemaphoreType.DMA
    return pl.pallas_call(
        functools.partial(kernel, dims),
        out_shape=jax.ShapeDtypeStruct((nb, points), jnp.float32),
        in_specs=[
            pl.BlockSpec(memory_space=pltpu.SMEM),
            pl.BlockSpec(memory_space=pl.ANY),
            pl.BlockSpec(memory_space=pl.ANY),
        ],
        out_specs=pl.BlockSpec(memory_space=pltpu.VMEM),
        scratch_shapes=[
            pltpu.VMEM((2 * bin_count, length), jnp.bfloat16),
            pltpu.VMEM((slots, chunk_segs, group, length), jnp.bfloat16),
            pltpu.VMEM((points, mics), jnp.int32),
            pltpu.VMEM((chunks, T * rows, mics_here), jnp.bfloat16),
            pltpu.VMEM((M, chunks * T * rows, mics_here), jnp.bfloat16),
            pltpu.VMEM((nb, 2, points, mics), jnp.bfloat16),
            pltpu.VMEM((nb * 2 * points, chunks * T * rows), jnp.float32),
            DMA((slots,)),
            DMA(()),
            DMA((chunks, peers)),
            DMA((chunks, max(Z - 1, 1))),
            DMA((chunks, M)),
        ],
        compiler_params=pltpu.CompilerParams(
            collective_id=0, has_side_effects=True, vmem_limit_bytes=56 * 1024 * 1024),
        cost_estimate=pl.CostEstimate(
            flops=2 * samples.size * 2 * bin_count, bytes_accessed=samples.size * 2, transcendentals=0),
    )(bin_ids, samples, delays)


def solution(mesh):
    placed = (P("tm", "mic", None), P(), P("mic", None))
    return jax.shard_map(
        functools.partial(per_device, mesh.shape["tm"], mesh.shape["mic"]),
        mesh=mesh, in_specs=placed, out_specs=P("tm", "mic"), check_vma=False)
```

```python
import functools
import math

import jax
import jax.numpy as jnp
import numpy as np
from jax import lax
from jax.experimental import pallas as pl
from jax.experimental.pallas import tpu as pltpu
from jax.sharding import PartitionSpec as P

MESH = pl.DeviceIdType.MESH
NT = (((1,), (1,)), ((), ()))


def fit(function, count):
    nodes = 0.125 + 0.125 * np.cos(np.pi * (np.arange(64) + 0.5) / 64)
    series = np.polynomial.chebyshev.Chebyshev.fit(nodes, function(np.sqrt(nodes)), count - 1, domain=[0, 0.25])
    return [float(c) for c in series.convert(kind=np.polynomial.Polynomial).coef]


SIN_HALF = fit(lambda r: np.sin(np.pi * r) / r, 5)
COS_HALF = fit(lambda r: np.cos(np.pi * r), 6)


def horner(coefficients, y):
    total = coefficients[-1]
    for c in coefficients[-2::-1]:
        total = total * y + c
    return total


def fraction(turns):
    return turns - ((turns + 12582912.0) - 12582912.0)


def cos_turns(turns):
    r = fraction(turns)
    s = r * horner(SIN_HALF, r * r)
    return 1.0 - (s + s) * s


def cos_sin_turns(turns):
    r = fraction(turns)
    y = r * r
    s = r * horner(SIN_HALF, y)
    twice = s + s
    return 1.0 - twice * s, twice * horner(COS_HALF, y)


def kernel(dims, bins, samples, delays, out, table, held, delay, quarter, other_delay, spec, gath, steer, acc,
           power_out, power_in, sample_sem, delay_sem, send_sem, fwd_sem, recv_sem, quarter_send, quarter_recv,
           power_sem):
    T, Z, Y, bin_count, nb, wb, rows, chunk_segs, parts, group, steps, slots = dims
    mics_here, length = samples.shape[1], samples.shape[2]
    points, mics = delays.shape
    seg_groups = steps // parts
    t, m = lax.axis_index("tm"), lax.axis_index("mic")
    z, y = lax.div(m, Y), lax.rem(m, Y)
    side = lax.rem(z, 2)

    def mic_of(z2, y2):
        return z2 * Y + y2

    def fetch(i, slot):
        c, q = lax.div(i, parts), lax.rem(i, parts)
        return pltpu.make_async_copy(
            samples.at[pl.ds(c * chunk_segs, chunk_segs), pl.ds(pl.multiple_of(q * group, group), group)],
            held.at[slot], sample_sem.at[slot])

    pltpu.make_async_copy(delays, delay, delay_sem).start()
    for i in range(min(slots, steps)):
        fetch(i, i).start()

    near = [(lax.rem(t + a, T), lax.rem(z + k, Z), y) for k in range(Z) for a in range(T) if k or a]
    across = [(lax.rem(t + a, T), z, 1 - y) for a in range(T)]
    peers = near + across
    partner = mic_of(z + 1 - 2 * side, y)
    barrier = pltpu.get_barrier_semaphore()
    for t2, z2, y2 in peers:
        pl.semaphore_signal(barrier, inc=1, device_id={"tm": t2, "mic": mic_of(z2, y2)}, device_id_type=MESH)

    table_rows = 2 * bin_count
    row = lax.broadcasted_iota(jnp.int32, (table_rows, 128), 0)
    lane = lax.broadcasted_iota(jnp.int32, (table_rows, 128), 1)
    bin_of = (row // (2 * wb)) * wb + row % wb
    scale = jnp.zeros((table_rows, 128), jnp.float32)
    for i in range(bin_count):
        scale = jnp.where(bin_of == i, bins[i].astype(jnp.float32) * (1.0 / length), scale)
    shift = jnp.where((row // wb) % 2 == 1, jnp.float32(0.25), jnp.float32(0.0))
    lane8 = lax.broadcasted_iota(jnp.int32, (8, 128), 1)

    def window_at(j, like):
        return 0.5 - 0.5 * cos_turns((like + j * 128).astype(jnp.float32) * (1.0 / length))

    def norm_step(j, total):
        w = window_at(j, lane8)
        return total + w * w

    norm = jnp.sum(lax.fori_loop(0, length // 128, norm_step, jnp.zeros((8, 128), jnp.float32), unroll=4),
                   axis=1, keepdims=True)[0:1]
    inverse = 1.0 / jnp.sqrt(norm)

    def table_step(j, carry):
        w = window_at(j, lane8)[0:1] * inverse
        turns = (lane + j * 128).astype(jnp.float32) * scale + shift
        table[:, pl.ds(pl.multiple_of(j * 128, 128), 128)] = (w * cos_turns(turns)).astype(jnp.bfloat16)
        return carry

    lax.fori_loop(0, length // 128, table_step, 0, unroll=4)

    own_scale = [bins[t * nb + side * wb + b].astype(jnp.float32) * (1.0 / length) for b in range(wb)]
    width = 512 if mics % 512 == 0 else 128
    share = points // T

    def block_of(i, m2):
        g, q = lax.div(i, parts), lax.rem(i, parts)
        return gath.at[m2, pl.ds(pl.multiple_of(g * T * rows, T * rows), T * rows),
                       pl.ds(pl.multiple_of(q * group, group), group)]

    def slot_of(i):
        g, q = lax.div(i, parts), lax.rem(i, parts)
        return gath.at[m, pl.ds(pl.multiple_of(g * T * rows + t * rows, rows), rows),
                       pl.ds(pl.multiple_of(q * group, group), group)]

    def source_of(i, t2, z2):
        worker = t2 * 2 + lax.rem(z2, 2)
        return spec.at[i, pl.ds(pl.multiple_of(worker * rows, rows), rows)]

    def push(i, index, t2, z2, y2):
        return pltpu.make_async_remote_copy(
            src_ref=source_of(i, t2, z2), dst_ref=slot_of(i),
            send_sem=send_sem.at[i, index], recv_sem=recv_sem.at[i, m],
            device_id={"tm": t2, "mic": mic_of(z2, y2)}, device_id_type=MESH)

    def forward(i, k):
        m2 = mic_of(lax.rem(z + k, Z), y)
        return pltpu.make_async_remote_copy(
            src_ref=block_of(i, m2), dst_ref=block_of(i, m2),
            send_sem=fwd_sem.at[i, k - 1], recv_sem=recv_sem.at[i, m2],
            device_id={"tm": t, "mic": mic_of(z, 1 - y)}, device_id_type=MESH)

    def arrived(i, m2):
        pltpu.make_async_copy(block_of(i, m2), block_of(i, m2), recv_sem.at[i, m2]).wait()

    def send_chunk(i):
        for index, peer in enumerate(peers):
            push(i, index, *peer).start()
        pltpu.make_async_copy(source_of(i, t, z), slot_of(i), recv_sem.at[i, m]).start()

    def pass_on(i):
        for k in range(1, Z):
            arrived(i, mic_of(lax.rem(z + k, Z), y))
            forward(i, k).start()

    def share_of(t2):
        return other_delay.at[pl.ds(pl.multiple_of(t2 * share, share), share)]

    def give_share():
        return pltpu.make_async_remote_copy(
            src_ref=quarter, dst_ref=share_of(t), send_sem=quarter_send.at[0], recv_sem=quarter_recv.at[t],
            device_id={"tm": t, "mic": partner}, device_id_type=MESH)

    def share_on(a):
        return pltpu.make_async_remote_copy(
            src_ref=share_of(t), dst_ref=share_of(t), send_sem=quarter_send.at[a], recv_sem=quarter_recv.at[t],
            device_id={"tm": lax.rem(t + a, T), "mic": m}, device_id_type=MESH)

    def share_arrived(t2):
        pltpu.make_async_copy(share_of(t2), share_of(t2), quarter_recv.at[t2]).wait()

    pltpu.make_async_copy(delays, delay, delay_sem).wait()
    quarter[...] = delay[pl.ds(pl.multiple_of(t * share, share), share), :].astype(jnp.int16)
    pl.semaphore_wait(barrier, len(peers))
    give_share().start()

    def step(i, carry):
        slot = lax.rem(i, slots)
        fetch(i, slot).wait()
        block = held[slot].reshape(chunk_segs * group, length)
        found = lax.dot_general(block, table[...], NT, preferred_element_type=jnp.float32)
        found = [found[s * group:(s + 1) * group].T for s in range(chunk_segs)]
        for worker in range(2 * T):
            lines = [f[worker * 2 * wb:(worker + 1) * 2 * wb] for f in found]
            spec[i, worker * rows:(worker + 1) * rows, :] = jnp.concatenate(lines, axis=0).astype(jnp.bfloat16)

        @pl.when(i + slots < steps)
        def _():
            fetch(i + slots, slot).start()

        send_chunk(i)

        @pl.when(i == 1)
        def _():
            share_arrived(t)
            for a in range(1, T):
                share_on(a).start()

        @pl.when(i >= 2)
        def _():
            pass_on(i - 2)

        return carry

    lax.fori_loop(0, steps, step, 0)

    piece = 16
    pieces = points // piece
    turn_of = {pieces // 8: steps - 2, pieces // 2: steps - 1}

    def steer_step(half, i):
        first = pl.multiple_of(i * piece, piece)
        source = other_delay if half else delay
        for start in range(0, mics, width):
            turns = source[pl.ds(first, piece), start:start + width].astype(jnp.int32).astype(jnp.float32)
            for b in range(wb):
                cosine, sine = cos_sin_turns(turns * own_scale[b])
                steer[b, 0, half, pl.ds(first, piece), start:start + width] = cosine.astype(jnp.bfloat16)
                steer[b, 1, half, pl.ds(first, piece), start:start + width] = sine.astype(jnp.bfloat16)

    def own_step(i, carry):
        steer_step(0, i)
        for turn, late in turn_of.items():
            @pl.when(i == turn)
            def _():
                pass_on(late)

        return carry

    def partner_step(i, carry):
        steer_step(1, i)
        return carry

    lax.fori_loop(0, pieces, own_step, 0)
    for a in range(1, T):
        share_arrived(lax.rem(t + a, T))
    lax.fori_loop(0, pieces, partner_step, 0)

    acc[...] = jnp.zeros_like(acc)

    def add_block(m2):
        columns = pl.ds(pl.multiple_of(m2 * mics_here, mics_here), mics_here)
        lhs = steer[:, :, :, :, columns].reshape(wb * 4 * points, mics_here)
        acc[...] += lax.dot_general(lhs, gath[m2], NT, preferred_element_type=jnp.float32)

    def own_y(k, carry):
        m2 = mic_of(lax.rem(z + k, Z), y)

        @pl.when(k == 0)
        def _():
            for i in range(steps):
                arrived(i, m2)

        add_block(m2)
        return carry

    lax.fori_loop(0, Z, own_y, 0)

    def other_y(k, carry):
        m2 = mic_of(lax.rem(z + k, Z), 1 - y)
        for i in range(steps):
            arrived(i, m2)
        add_block(m2)
        return carry

    lax.fori_loop(0, Z, other_y, 0)

    columns = seg_groups * T * rows
    column = lax.broadcasted_iota(jnp.int32, (2 * points, columns), 1)
    own, theirs = [], []
    for b in range(wb):
        along_cos = acc[(4 * b) * points:(4 * b + 2) * points]
        along_sin = acc[(4 * b + 2) * points:(4 * b + 4) * points]
        real = along_cos - pltpu.roll(along_sin, columns - wb, axis=1)
        imag = pltpu.roll(along_cos, columns - wb, axis=1) + along_sin
        power = jnp.where(column % (2 * wb) == b, real * real + imag * imag, 0.0)
        total = jnp.sum(power.T, axis=0, keepdims=True) * (1.0 / (mics * seg_groups * chunk_segs * T))
        own.append(total[:, :points])
        theirs.append(total[:, points:])
    power_out[...] = jnp.zeros_like(power_out)
    power_out[0:wb, :] = jnp.concatenate(theirs, axis=0)
    swap = pltpu.make_async_remote_copy(
        src_ref=power_out, dst_ref=power_in, send_sem=power_sem.at[0], recv_sem=power_sem.at[1],
        device_id={"tm": t, "mic": partner}, device_id_type=MESH)
    swap.start()

    def drain(i, carry):
        for index, peer in enumerate(peers):
            push(i, index, *peer).wait_send()
        for k in range(1, Z):
            forward(i, k).wait_send()
        return carry

    lax.fori_loop(0, steps, drain, 0)
    give_share().wait_send()
    for a in range(1, T):
        share_on(a).wait_send()
    swap.wait()
    own = jnp.concatenate(own, axis=0)
    came = power_in[0:wb, :]
    out[0:wb, :] = jnp.where(side == 0, own, came)
    out[wb:2 * wb, :] = jnp.where(side == 0, came, own)


def per_device(T, M, samples, bin_ids, delays):
    segs, mics_here, length = samples.shape
    points, mics = delays.shape
    bin_count = bin_ids.shape[0]
    Y = 2
    Z = M // Y
    nb = bin_count // T
    wb = nb // 2
    chunk_segs = max(1, 16 // (2 * wb))
    rows = chunk_segs * 2 * wb
    group = min(mics_here, 256)
    parts = mics_here // group
    steps = segs // chunk_segs * parts
    slots = min(steps, 3)
    columns = segs // chunk_segs * T * rows
    peers = T * Z - 1 + T
    dims = (T, Z, Y, bin_count, nb, wb, rows, chunk_segs, parts, group, steps, slots)
    DMA = pltpu.SemaphoreType.DMA
    return pl.pallas_call(
        functools.partial(kernel, dims),
        out_shape=jax.ShapeDtypeStruct((nb, points), jnp.float32),
        in_specs=[
            pl.BlockSpec(memory_space=pltpu.SMEM),
            pl.BlockSpec(memory_space=pl.ANY),
            pl.BlockSpec(memory_space=pl.ANY),
        ],
        out_specs=pl.BlockSpec(memory_space=pltpu.VMEM),
        scratch_shapes=[
            pltpu.VMEM((2 * bin_count, length), jnp.bfloat16),
            pltpu.VMEM((slots, chunk_segs, group, length), jnp.bfloat16),
            pltpu.VMEM((points, mics), jnp.int32),
            pltpu.VMEM((points // T, mics), jnp.int16),
            pltpu.VMEM((points, mics), jnp.int16),
            pltpu.VMEM((steps, 2 * T * rows, group), jnp.bfloat16),
            pltpu.VMEM((M, columns, mics_here), jnp.bfloat16),
            pltpu.VMEM((wb, 2, 2, points, mics), jnp.bfloat16),
            pltpu.VMEM((wb * 4 * points, columns), jnp.float32),
            pltpu.VMEM((8, points), jnp.float32),
            pltpu.VMEM((8, points), jnp.float32),
            DMA((slots,)),
            DMA(()),
            DMA((steps, peers)),
            DMA((steps, Z - 1)),
            DMA((steps, M)),
            DMA((T,)),
            DMA((T,)),
            DMA((2,)),
        ],
        compiler_params=pltpu.CompilerParams(
            collective_id=0, has_side_effects=True, vmem_limit_bytes=56 * 1024 * 1024),
        cost_estimate=pl.CostEstimate(
            flops=2 * samples.size * 2 * bin_count, bytes_accessed=samples.size * 2, transcendentals=0),
    )(bin_ids, samples, delays)


def solution(mesh):
    placed = (P("tm", "mic", None), P(), P("mic", None))
    return jax.shard_map(
        functools.partial(per_device, mesh.shape["tm"], mesh.shape["mic"]),
        mesh=mesh, in_specs=placed, out_specs=P("tm", "mic"), check_vma=False)
```

```python
import functools
import math

import jax
import jax.numpy as jnp
import numpy as np
from jax import lax
from jax.experimental import pallas as pl
from jax.experimental.pallas import tpu as pltpu
from jax.sharding import PartitionSpec as P

MESH = pl.DeviceIdType.MESH
NT = (((1,), (1,)), ((), ()))


def fit(function, count):
    nodes = 0.125 + 0.125 * np.cos(np.pi * (np.arange(64) + 0.5) / 64)
    series = np.polynomial.chebyshev.Chebyshev.fit(nodes, function(np.sqrt(nodes)), count - 1, domain=[0, 0.25])
    return [float(c) for c in series.convert(kind=np.polynomial.Polynomial).coef]


SIN_HALF = fit(lambda r: math.sqrt(2) * np.sin(np.pi * r) / r, 5)
COS_HALF = fit(lambda r: math.sqrt(2) * np.cos(np.pi * r), 5)


def horner(coefficients, y):
    total = coefficients[-1]
    for c in coefficients[-2::-1]:
        total = total * y + c
    return total


def fraction(turns):
    return turns - ((turns + 12582912.0) - 12582912.0)


def cos_turns(turns):
    r = fraction(turns)
    s = r * horner(SIN_HALF, r * r)
    return 1.0 - s * s


def cos_sin_turns(turns):
    r = fraction(turns)
    y = r * r
    s = r * horner(SIN_HALF, y)
    return 1.0 - s * s, s * horner(COS_HALF, y)


def kernel(dims, bins, samples, delays, out, table, held, delay, quarter, other_delay, spec, gath, steer, acc,
           power_out, power_in, sample_sem, delay_sem, send_sem, fwd_sem, recv_sem, quarter_send, quarter_recv,
           power_sem):
    T, Z, Y, bin_count, nb, wb, rows, chunk_segs, parts, group, steps, slots = dims
    mics_here, length = samples.shape[1], samples.shape[2]
    points, mics = delays.shape
    seg_groups = steps // parts
    t, m = lax.axis_index("tm"), lax.axis_index("mic")
    z, y = lax.div(m, Y), lax.rem(m, Y)
    side = lax.rem(z, 2)

    def mic_of(z2, y2):
        return z2 * Y + y2

    def fetch(i, slot):
        c, q = lax.div(i, parts), lax.rem(i, parts)
        return pltpu.make_async_copy(
            samples.at[pl.ds(c * chunk_segs, chunk_segs), pl.ds(pl.multiple_of(q * group, group), group)],
            held.at[slot], sample_sem.at[slot])

    pltpu.make_async_copy(delays, delay, delay_sem).start()
    for i in range(min(slots, steps)):
        fetch(i, i).start()

    near = [(lax.rem(t + a, T), lax.rem(z + k, Z), y) for k in range(Z) for a in range(T) if k or a]
    across = [(lax.rem(t + a, T), z, 1 - y) for a in range(T)]
    peers = near + across
    partner = mic_of(z + 1 - 2 * side, y)
    barrier = pltpu.get_barrier_semaphore()
    for t2, z2, y2 in peers:
        pl.semaphore_signal(barrier, inc=1, device_id={"tm": t2, "mic": mic_of(z2, y2)}, device_id_type=MESH)

    table_rows = 2 * bin_count
    row = lax.broadcasted_iota(jnp.int32, (table_rows, 128), 0)
    lane = lax.broadcasted_iota(jnp.int32, (table_rows, 128), 1)
    bin_of = (row // (2 * wb)) * wb + row % wb
    scale = jnp.zeros((table_rows, 128), jnp.float32)
    for i in range(bin_count):
        scale = jnp.where(bin_of == i, bins[i].astype(jnp.float32) * (1.0 / length), scale)
    shift = jnp.where((row // wb) % 2 == 1, jnp.float32(0.25), jnp.float32(0.0))
    lane8 = lax.broadcasted_iota(jnp.int32, (8, 128), 1)

    def window_at(j, like):
        return 0.5 - 0.5 * cos_turns((like + j * 128).astype(jnp.float32) * (1.0 / length))

    def norm_step(j, total):
        w = window_at(j, lane8)
        return total + w * w

    norm = jnp.sum(lax.fori_loop(0, length // 128, norm_step, jnp.zeros((8, 128), jnp.float32), unroll=4),
                   axis=1, keepdims=True)[0:1]
    inverse = 1.0 / jnp.sqrt(norm)

    def table_step(j, carry):
        w = window_at(j, lane8)[0:1] * inverse
        turns = (lane + j * 128).astype(jnp.float32) * scale + shift
        table[:, pl.ds(pl.multiple_of(j * 128, 128), 128)] = (w * cos_turns(turns)).astype(jnp.bfloat16)
        return carry

    lax.fori_loop(0, length // 128, table_step, 0, unroll=4)

    own_scale = [bins[t * nb + side * wb + b].astype(jnp.float32) * (1.0 / length) for b in range(wb)]
    width = 512 if mics % 512 == 0 else 128
    share = points // T

    def block_of(i, m2):
        g, q = lax.div(i, parts), lax.rem(i, parts)
        return gath.at[m2, pl.ds(pl.multiple_of(g * T * rows, T * rows), T * rows),
                       pl.ds(pl.multiple_of(q * group, group), group)]

    def slot_of(i):
        g, q = lax.div(i, parts), lax.rem(i, parts)
        return gath.at[m, pl.ds(pl.multiple_of(g * T * rows + t * rows, rows), rows),
                       pl.ds(pl.multiple_of(q * group, group), group)]

    def source_of(i, t2, z2):
        worker = t2 * 2 + lax.rem(z2, 2)
        return spec.at[i, pl.ds(pl.multiple_of(worker * rows, rows), rows)]

    def push(i, index, t2, z2, y2):
        return pltpu.make_async_remote_copy(
            src_ref=source_of(i, t2, z2), dst_ref=slot_of(i),
            send_sem=send_sem.at[i, index], recv_sem=recv_sem.at[i, m],
            device_id={"tm": t2, "mic": mic_of(z2, y2)}, device_id_type=MESH)

    def forward(i, k):
        m2 = mic_of(lax.rem(z + k, Z), y)
        return pltpu.make_async_remote_copy(
            src_ref=block_of(i, m2), dst_ref=block_of(i, m2),
            send_sem=fwd_sem.at[i, k - 1], recv_sem=recv_sem.at[i, m2],
            device_id={"tm": t, "mic": mic_of(z, 1 - y)}, device_id_type=MESH)

    def arrived(i, m2):
        pltpu.make_async_copy(block_of(i, m2), block_of(i, m2), recv_sem.at[i, m2]).wait()

    def send_chunk(i):
        for index, peer in enumerate(peers):
            push(i, index, *peer).start()
        pltpu.make_async_copy(source_of(i, t, z), slot_of(i), recv_sem.at[i, m]).start()

    def pass_on(i):
        for k in range(1, Z):
            arrived(i, mic_of(lax.rem(z + k, Z), y))
            forward(i, k).start()

    def share_of(t2):
        return other_delay.at[pl.ds(pl.multiple_of(t2 * share, share), share)]

    def give_share():
        return pltpu.make_async_remote_copy(
            src_ref=quarter, dst_ref=share_of(t), send_sem=quarter_send.at[0], recv_sem=quarter_recv.at[t],
            device_id={"tm": t, "mic": partner}, device_id_type=MESH)

    def share_on(a):
        return pltpu.make_async_remote_copy(
            src_ref=share_of(t), dst_ref=share_of(t), send_sem=quarter_send.at[a], recv_sem=quarter_recv.at[t],
            device_id={"tm": lax.rem(t + a, T), "mic": m}, device_id_type=MESH)

    def share_arrived(t2):
        pltpu.make_async_copy(share_of(t2), share_of(t2), quarter_recv.at[t2]).wait()

    pltpu.make_async_copy(delays, delay, delay_sem).wait()
    quarter[...] = delay[pl.ds(pl.multiple_of(t * share, share), share), :].astype(jnp.int16)
    pl.semaphore_wait(barrier, len(peers))
    give_share().start()

    def trig(half, first, count, start):
        source = other_delay if half else delay
        turns = source[pl.ds(first, count), start:start + width].astype(jnp.int32).astype(jnp.float32)
        for b in range(wb):
            cosine, sine = cos_sin_turns(turns * own_scale[b])
            steer[half, b, 0, pl.ds(first, count), start:start + width] = cosine.astype(jnp.bfloat16)
            steer[half, b, 1, pl.ds(first, count), start:start + width] = sine.astype(jnp.bfloat16)

    piece = 16

    def trig_pieces(half, first, count):
        return [functools.partial(trig, half, pl.multiple_of(first + lead, piece), piece, start)
                for lead in range(0, count, piece) for start in range(0, mics, width)]

    at_once = 2 if chunk_segs % 2 == 0 else 1
    slices = chunk_segs // at_once
    points_step = points // steps

    def step(i, carry):
        slot = lax.rem(i, slots)
        fetch(i, slot).wait()
        todo = trig_pieces(0, pl.multiple_of(i * points_step, points_step), points_step)
        found = []
        for n in range(slices):
            block = held[slot, n * at_once:(n + 1) * at_once].reshape(at_once * group, length)
            part = lax.dot_general(block, table[...], NT, preferred_element_type=jnp.float32)
            for work in todo[n * len(todo) // slices:(n + 1) * len(todo) // slices]:
                work()
            found += [part[s * group:(s + 1) * group].T for s in range(at_once)]
        for worker in range(2 * T):
            lines = [f[worker * 2 * wb:(worker + 1) * 2 * wb] for f in found]
            spec[i, worker * rows:(worker + 1) * rows, :] = jnp.concatenate(lines, axis=0).astype(jnp.bfloat16)

        @pl.when(i + slots < steps)
        def _():
            fetch(i + slots, slot).start()

        send_chunk(i)

        @pl.when(i == 1)
        def _():
            share_arrived(t)
            for a in range(1, T):
                share_on(a).start()

        @pl.when(i >= 2)
        def _():
            pass_on(i - 2)

        return carry

    lax.fori_loop(0, steps, step, 0)

    acc[...] = jnp.zeros_like(acc)
    for a in range(1, T):
        share_arrived(lax.rem(t + a, T))

    def add_block(half, m2):
        columns = pl.ds(pl.multiple_of(m2 * mics_here, mics_here), mics_here)
        lhs = steer[half, :, :, :, columns].reshape(wb * 2 * points, mics_here)
        acc[half] += lax.dot_general(lhs, gath[m2], NT, preferred_element_type=jnp.float32)

    trig_blocks = points // piece
    each = -(-trig_blocks // Z)

    def own_points(k, carry):
        m2 = mic_of(lax.rem(z + k, Z), y)

        @pl.when(k == 0)
        def _():
            pass_on(steps - 2)
            for i in range(steps):
                arrived(i, m2)

        @pl.when(k == 1)
        def _():
            pass_on(steps - 1)

        add_block(0, m2)
        for n in range(each):
            block = jnp.minimum(k * each + n, trig_blocks - 1)
            for work in trig_pieces(1, pl.multiple_of(block * piece, piece), piece):
                work()
        return carry

    lax.fori_loop(0, Z, own_points, 0)

    def partner_points(k, carry):
        add_block(1, mic_of(lax.rem(z + k, Z), y))
        return carry

    lax.fori_loop(0, Z, partner_points, 0)

    def other_y(k, carry):
        m2 = mic_of(lax.rem(z + k, Z), 1 - y)
        for i in range(steps):
            arrived(i, m2)
        add_block(0, m2)
        add_block(1, m2)
        return carry

    lax.fori_loop(0, Z, other_y, 0)

    columns = seg_groups * T * rows
    column = lax.broadcasted_iota(jnp.int32, (points, columns), 1)
    totals = []
    for half in range(2):
        lines = []
        for b in range(wb):
            along_cos = acc[half, (2 * b) * points:(2 * b + 1) * points]
            along_sin = acc[half, (2 * b + 1) * points:(2 * b + 2) * points]
            real = along_cos - pltpu.roll(along_sin, columns - wb, axis=1)
            imag = pltpu.roll(along_cos, columns - wb, axis=1) + along_sin
            power = jnp.where(column % (2 * wb) == b, real * real + imag * imag, 0.0)
            lines.append(jnp.sum(power.T, axis=0, keepdims=True))
        totals.append(jnp.concatenate(lines, axis=0) * (1.0 / (mics * seg_groups * chunk_segs * T)))
    own, theirs = totals
    power_out[...] = jnp.zeros_like(power_out)
    power_out[0:wb, :] = theirs
    swap = pltpu.make_async_remote_copy(
        src_ref=power_out, dst_ref=power_in, send_sem=power_sem.at[0], recv_sem=power_sem.at[1],
        device_id={"tm": t, "mic": partner}, device_id_type=MESH)
    swap.start()

    def drain(i, carry):
        for index, peer in enumerate(peers):
            push(i, index, *peer).wait_send()
        for k in range(1, Z):
            forward(i, k).wait_send()
        return carry

    lax.fori_loop(0, steps, drain, 0)
    give_share().wait_send()
    for a in range(1, T):
        share_on(a).wait_send()
    swap.wait()
    came = power_in[0:wb, :]
    out[0:wb, :] = jnp.where(side == 0, own, came)
    out[wb:2 * wb, :] = jnp.where(side == 0, came, own)


def per_device(T, M, samples, bin_ids, delays):
    segs, mics_here, length = samples.shape
    points, mics = delays.shape
    bin_count = bin_ids.shape[0]
    Y = 2
    Z = M // Y
    nb = bin_count // T
    wb = nb // 2
    chunk_segs = max(1, 16 // (2 * wb))
    rows = chunk_segs * 2 * wb
    group = min(mics_here, 256)
    parts = mics_here // group
    steps = segs // chunk_segs * parts
    slots = min(steps, 3)
    columns = segs // chunk_segs * T * rows
    peers = T * Z - 1 + T
    dims = (T, Z, Y, bin_count, nb, wb, rows, chunk_segs, parts, group, steps, slots)
    DMA = pltpu.SemaphoreType.DMA
    return pl.pallas_call(
        functools.partial(kernel, dims),
        out_shape=jax.ShapeDtypeStruct((nb, points), jnp.float32),
        in_specs=[
            pl.BlockSpec(memory_space=pltpu.SMEM),
            pl.BlockSpec(memory_space=pl.ANY),
            pl.BlockSpec(memory_space=pl.ANY),
        ],
        out_specs=pl.BlockSpec(memory_space=pltpu.VMEM),
        scratch_shapes=[
            pltpu.VMEM((2 * bin_count, length), jnp.bfloat16),
            pltpu.VMEM((slots, chunk_segs, group, length), jnp.bfloat16),
            pltpu.VMEM((points, mics), jnp.int32),
            pltpu.VMEM((points // T, mics), jnp.int16),
            pltpu.VMEM((points, mics), jnp.int16),
            pltpu.VMEM((steps, 2 * T * rows, group), jnp.bfloat16),
            pltpu.VMEM((M, columns, mics_here), jnp.bfloat16),
            pltpu.VMEM((2, wb, 2, points, mics), jnp.bfloat16),
            pltpu.VMEM((2, wb * 2 * points, columns), jnp.float32),
            pltpu.VMEM((8, points), jnp.float32),
            pltpu.VMEM((8, points), jnp.float32),
            DMA((slots,)),
            DMA(()),
            DMA((steps, peers)),
            DMA((steps, Z - 1)),
            DMA((steps, M)),
            DMA((T,)),
            DMA((T,)),
            DMA((2,)),
        ],
        compiler_params=pltpu.CompilerParams(
            collective_id=0, has_side_effects=True, vmem_limit_bytes=56 * 1024 * 1024),
        cost_estimate=pl.CostEstimate(
            flops=2 * samples.size * 2 * bin_count, bytes_accessed=samples.size * 2, transcendentals=0),
    )(bin_ids, samples, delays)


def solution(mesh):
    placed = (P("tm", "mic", None), P(), P("mic", None))
    return jax.shard_map(
        functools.partial(per_device, mesh.shape["tm"], mesh.shape["mic"]),
        mesh=mesh, in_specs=placed, out_specs=P("tm", "mic"), check_vma=False)
```

```python
import functools
import math

import jax
import jax.numpy as jnp
import numpy as np
from jax import lax
from jax.experimental import pallas as pl
from jax.experimental.pallas import tpu as pltpu
from jax.sharding import PartitionSpec as P

MESH = pl.DeviceIdType.MESH
NT = (((1,), (1,)), ((), ()))


def fit(function, count):
    nodes = 0.125 + 0.125 * np.cos(np.pi * (np.arange(64) + 0.5) / 64)
    series = np.polynomial.chebyshev.Chebyshev.fit(nodes, function(np.sqrt(nodes)), count - 1, domain=[0, 0.25])
    return [float(c) for c in series.convert(kind=np.polynomial.Polynomial).coef]


SIN_HALF = fit(lambda r: math.sqrt(2) * np.sin(np.pi * r) / r, 5)
COS_HALF = fit(lambda r: math.sqrt(2) * np.cos(np.pi * r), 5)


def horner(coefficients, y):
    total = coefficients[-1]
    for c in coefficients[-2::-1]:
        total = total * y + c
    return total


def fraction(turns):
    return turns - ((turns + 12582912.0) - 12582912.0)


def cos_turns(turns):
    r = fraction(turns)
    s = r * horner(SIN_HALF, r * r)
    return 1.0 - s * s


def cos_sin_turns(turns):
    r = fraction(turns)
    y = r * r
    s = r * horner(SIN_HALF, y)
    return 1.0 - s * s, s * horner(COS_HALF, y)


def kernel(dims, bins, samples, delays, out, table, held, delay, quarter, other_delay, spec, gath, steer, acc,
           power_out, power_in, sample_sem, delay_sem, send_sem, fwd_sem, recv_sem, quarter_send, quarter_recv,
           power_sem):
    T, Z, Y, bin_count, nb, wb, rows, chunk_segs, parts, group, steps, slots = dims
    mics_here, length = samples.shape[1], samples.shape[2]
    points, mics = delays.shape
    seg_groups = steps // parts
    t, m = lax.axis_index("tm"), lax.axis_index("mic")
    z, y = lax.div(m, Y), lax.rem(m, Y)
    side = lax.rem(z, 2)

    def mic_of(z2, y2):
        return z2 * Y + y2

    def fetch(i, slot):
        c, q = lax.div(i, parts), lax.rem(i, parts)
        return pltpu.make_async_copy(
            samples.at[pl.ds(c * chunk_segs, chunk_segs), pl.ds(pl.multiple_of(q * group, group), group)],
            held.at[slot], sample_sem.at[slot])

    pltpu.make_async_copy(delays, delay, delay_sem).start()
    for i in range(min(slots, steps)):
        fetch(i, i).start()

    near = [(lax.rem(t + a, T), lax.rem(z + k, Z), y) for k in range(Z) for a in range(T) if k or a]
    across = [(lax.rem(t + a, T), z, 1 - y) for a in range(T)]
    peers = near + across
    partner = mic_of(z + 1 - 2 * side, y)
    barrier = pltpu.get_barrier_semaphore()
    for t2, z2, y2 in peers:
        pl.semaphore_signal(barrier, inc=1, device_id={"tm": t2, "mic": mic_of(z2, y2)}, device_id_type=MESH)

    table_rows = 2 * bin_count
    row = lax.broadcasted_iota(jnp.int32, (table_rows, 128), 0)
    lane = lax.broadcasted_iota(jnp.int32, (table_rows, 128), 1)
    bin_of = (row // (2 * wb)) * wb + row % wb
    scale = jnp.zeros((table_rows, 128), jnp.float32)
    for i in range(bin_count):
        scale = jnp.where(bin_of == i, bins[i].astype(jnp.float32) * (1.0 / length), scale)
    shift = jnp.where((row // wb) % 2 == 1, jnp.float32(0.25), jnp.float32(0.0))
    lane8 = lax.broadcasted_iota(jnp.int32, (8, 128), 1)

    def window_at(j, like):
        return 0.5 - 0.5 * cos_turns((like + j * 128).astype(jnp.float32) * (1.0 / length))

    def norm_step(j, total):
        w = window_at(j, lane8)
        return total + w * w

    norm = jnp.sum(lax.fori_loop(0, length // 128, norm_step, jnp.zeros((8, 128), jnp.float32), unroll=4),
                   axis=1, keepdims=True)[0:1]
    inverse = 1.0 / jnp.sqrt(norm)

    def table_step(j, carry):
        w = window_at(j, lane8)[0:1] * inverse
        turns = (lane + j * 128).astype(jnp.float32) * scale + shift
        table[:, pl.ds(pl.multiple_of(j * 128, 128), 128)] = (w * cos_turns(turns)).astype(jnp.bfloat16)
        return carry

    lax.fori_loop(0, length // 128, table_step, 0, unroll=4)

    own_scale = [bins[t * nb + side * wb + b].astype(jnp.float32) * (1.0 / length) for b in range(wb)]
    width = 512 if mics % 512 == 0 else 128
    share = points // T

    def block_of(g, m2):
        return gath.at[m2, pl.ds(pl.multiple_of(g * T * rows, T * rows), T * rows)]

    def slot_of(g):
        return gath.at[m, pl.ds(pl.multiple_of(g * T * rows + t * rows, rows), rows)]

    def source_of(i, t2, z2):
        worker = t2 * 2 + lax.rem(z2, 2)
        return spec.at[i, pl.ds(pl.multiple_of(worker * rows, rows), rows)]

    def push(i, index, t2, z2, y2):
        return pltpu.make_async_remote_copy(
            src_ref=source_of(i, t2, z2), dst_ref=slot_of(i),
            send_sem=send_sem.at[i, index], recv_sem=recv_sem.at[i, m],
            device_id={"tm": t2, "mic": mic_of(z2, y2)}, device_id_type=MESH)

    def forward(i, k):
        m2 = mic_of(lax.rem(z + k, Z), y)
        return pltpu.make_async_remote_copy(
            src_ref=block_of(i, m2), dst_ref=block_of(i, m2),
            send_sem=fwd_sem.at[i, k - 1], recv_sem=recv_sem.at[i, m2],
            device_id={"tm": t, "mic": mic_of(z, 1 - y)}, device_id_type=MESH)

    def arrived(i, m2):
        pltpu.make_async_copy(block_of(i, m2), block_of(i, m2), recv_sem.at[i, m2]).wait()

    def send_chunk(i):
        for index, peer in enumerate(peers):
            push(i, index, *peer).start()
        pltpu.make_async_copy(source_of(i, t, z), slot_of(i), recv_sem.at[i, m]).start()

    def pass_on(i):
        for k in range(1, Z):
            arrived(i, mic_of(lax.rem(z + k, Z), y))
            forward(i, k).start()

    def share_of(t2):
        return other_delay.at[pl.ds(pl.multiple_of(t2 * share, share), share)]

    def give_share():
        return pltpu.make_async_remote_copy(
            src_ref=quarter, dst_ref=share_of(t), send_sem=quarter_send.at[0], recv_sem=quarter_recv.at[t],
            device_id={"tm": t, "mic": partner}, device_id_type=MESH)

    def share_on(a):
        return pltpu.make_async_remote_copy(
            src_ref=share_of(t), dst_ref=share_of(t), send_sem=quarter_send.at[a], recv_sem=quarter_recv.at[t],
            device_id={"tm": lax.rem(t + a, T), "mic": m}, device_id_type=MESH)

    def share_arrived(t2):
        pltpu.make_async_copy(share_of(t2), share_of(t2), quarter_recv.at[t2]).wait()

    pltpu.make_async_copy(delays, delay, delay_sem).wait()
    quarter[...] = delay[pl.ds(pl.multiple_of(t * share, share), share), :].astype(jnp.int16)
    pl.semaphore_wait(barrier, len(peers))
    give_share().start()

    def trig(half, first, count, start):
        source = other_delay if half else delay
        turns = source[pl.ds(first, count), start:start + width].astype(jnp.int32).astype(jnp.float32)
        for b in range(wb):
            cosine, sine = cos_sin_turns(turns * own_scale[b])
            steer[half, b, 0, pl.ds(first, count), start:start + width] = cosine.astype(jnp.bfloat16)
            steer[half, b, 1, pl.ds(first, count), start:start + width] = sine.astype(jnp.bfloat16)

    piece = 16

    def trig_pieces(half, first, count):
        return [functools.partial(trig, half, pl.multiple_of(first + lead, piece), piece, start)
                for lead in range(0, count, piece) for start in range(0, mics, width)]

    def step(i, carry):
        slot = lax.rem(i, slots)
        g, q = lax.div(i, parts), lax.rem(i, parts)
        fetch(i, slot).wait()
        block = held[slot].reshape(chunk_segs * group, length)
        found = lax.dot_general(block, table[...], NT, preferred_element_type=jnp.float32)
        found = [found[s * group:(s + 1) * group].T for s in range(chunk_segs)]
        for worker in range(2 * T):
            lines = [f[worker * 2 * wb:(worker + 1) * 2 * wb] for f in found]
            spec[g, worker * rows:(worker + 1) * rows, pl.ds(pl.multiple_of(q * group, group), group)] = (
                jnp.concatenate(lines, axis=0).astype(jnp.bfloat16))

        @pl.when(i + slots < steps)
        def _():
            fetch(i + slots, slot).start()

        @pl.when(q == parts - 1)
        def _():
            send_chunk(g)

        @pl.when(i == 1)
        def _():
            share_arrived(t)
            for a in range(1, T):
                share_on(a).start()

        return carry

    lax.fori_loop(0, steps, step, 0)

    acc[...] = jnp.zeros_like(acc)

    def add_block(half, m2):
        columns = pl.ds(pl.multiple_of(m2 * mics_here, mics_here), mics_here)
        lhs = steer[half, :, :, :, columns].reshape(wb * 2 * points, mics_here)
        acc[half] += lax.dot_general(lhs, gath[m2], NT, preferred_element_type=jnp.float32)

    def own_trig(i, carry):
        for work in trig_pieces(0, pl.multiple_of(i * piece, piece), piece):
            work()

        @pl.when(i == 0)
        def _():
            for g in range(seg_groups - 1):
                pass_on(g)

        return carry

    def partner_trig(i, carry):
        for work in trig_pieces(1, pl.multiple_of(i * piece, piece), piece):
            work()
        return carry

    def own_points(k, carry):
        m2 = mic_of(lax.rem(z + k, Z), y)

        @pl.when(k == 0)
        def _():
            pass_on(seg_groups - 1)
            for g in range(seg_groups):
                arrived(g, m2)

        add_block(0, m2)
        return carry

    lax.fori_loop(0, points // piece, own_trig, 0)
    lax.fori_loop(0, Z, own_points, 0)
    for a in range(1, T):
        share_arrived(lax.rem(t + a, T))
    lax.fori_loop(0, points // piece, partner_trig, 0)

    def partner_points(k, carry):
        add_block(1, mic_of(lax.rem(z + k, Z), y))
        return carry

    lax.fori_loop(0, Z, partner_points, 0)

    def other_y(k, carry):
        m2 = mic_of(lax.rem(z + k, Z), 1 - y)
        for g in range(seg_groups):
            arrived(g, m2)
        add_block(0, m2)
        add_block(1, m2)
        return carry

    lax.fori_loop(0, Z, other_y, 0)

    columns = seg_groups * T * rows
    column = lax.broadcasted_iota(jnp.int32, (points, columns), 1)
    totals = []
    for half in range(2):
        lines = []
        for b in range(wb):
            along_cos = acc[half, (2 * b) * points:(2 * b + 1) * points]
            along_sin = acc[half, (2 * b + 1) * points:(2 * b + 2) * points]
            real = along_cos - pltpu.roll(along_sin, columns - wb, axis=1)
            imag = pltpu.roll(along_cos, columns - wb, axis=1) + along_sin
            power = jnp.where(column % (2 * wb) == b, real * real + imag * imag, 0.0)
            lines.append(jnp.sum(power.T, axis=0, keepdims=True))
        totals.append(jnp.concatenate(lines, axis=0) * (1.0 / (mics * seg_groups * chunk_segs * T)))
    own, theirs = totals
    power_out[...] = jnp.zeros_like(power_out)
    power_out[0:wb, :] = theirs
    swap = pltpu.make_async_remote_copy(
        src_ref=power_out, dst_ref=power_in, send_sem=power_sem.at[0], recv_sem=power_sem.at[1],
        device_id={"tm": t, "mic": partner}, device_id_type=MESH)
    swap.start()

    def drain(i, carry):
        for index, peer in enumerate(peers):
            push(i, index, *peer).wait_send()
        for k in range(1, Z):
            forward(i, k).wait_send()
        return carry

    lax.fori_loop(0, seg_groups, drain, 0)
    give_share().wait_send()
    for a in range(1, T):
        share_on(a).wait_send()
    swap.wait()
    came = power_in[0:wb, :]
    out[0:wb, :] = jnp.where(side == 0, own, came)
    out[wb:2 * wb, :] = jnp.where(side == 0, came, own)


def per_device(T, M, samples, bin_ids, delays):
    segs, mics_here, length = samples.shape
    points, mics = delays.shape
    bin_count = bin_ids.shape[0]
    Y = 2
    Z = M // Y
    nb = bin_count // T
    wb = nb // 2
    chunk_segs = max(1, 16 // (2 * wb))
    rows = chunk_segs * 2 * wb
    group = min(mics_here, 256)
    parts = mics_here // group
    groups = segs // chunk_segs
    steps = groups * parts
    slots = min(steps, 3)
    columns = groups * T * rows
    peers = T * Z - 1 + T
    dims = (T, Z, Y, bin_count, nb, wb, rows, chunk_segs, parts, group, steps, slots)
    DMA = pltpu.SemaphoreType.DMA
    return pl.pallas_call(
        functools.partial(kernel, dims),
        out_shape=jax.ShapeDtypeStruct((nb, points), jnp.float32),
        in_specs=[
            pl.BlockSpec(memory_space=pltpu.SMEM),
            pl.BlockSpec(memory_space=pl.ANY),
            pl.BlockSpec(memory_space=pl.ANY),
        ],
        out_specs=pl.BlockSpec(memory_space=pltpu.VMEM),
        scratch_shapes=[
            pltpu.VMEM((2 * bin_count, length), jnp.bfloat16),
            pltpu.VMEM((slots, chunk_segs, group, length), jnp.bfloat16),
            pltpu.VMEM((points, mics), jnp.int32),
            pltpu.VMEM((points // T, mics), jnp.int16),
            pltpu.VMEM((points, mics), jnp.int16),
            pltpu.VMEM((groups, 2 * T * rows, mics_here), jnp.bfloat16),
            pltpu.VMEM((M, columns, mics_here), jnp.bfloat16),
            pltpu.VMEM((2, wb, 2, points, mics), jnp.bfloat16),
            pltpu.VMEM((2, wb * 2 * points, columns), jnp.float32),
            pltpu.VMEM((8, points), jnp.float32),
            pltpu.VMEM((8, points), jnp.float32),
            DMA((slots,)),
            DMA(()),
            DMA((groups, peers)),
            DMA((groups, Z - 1)),
            DMA((groups, M)),
            DMA((T,)),
            DMA((T,)),
            DMA((2,)),
        ],
        compiler_params=pltpu.CompilerParams(
            collective_id=0, has_side_effects=True, vmem_limit_bytes=56 * 1024 * 1024),
        cost_estimate=pl.CostEstimate(
            flops=2 * samples.size * 2 * bin_count, bytes_accessed=samples.size * 2, transcendentals=0),
    )(bin_ids, samples, delays)


def solution(mesh):
    placed = (P("tm", "mic", None), P(), P("mic", None))
    return jax.shard_map(
        functools.partial(per_device, mesh.shape["tm"], mesh.shape["mic"]),
        mesh=mesh, in_specs=placed, out_specs=P("tm", "mic"), check_vma=False)
```

```python
import functools
import math

import jax
import jax.numpy as jnp
import numpy as np
from jax import lax
from jax.experimental import pallas as pl
from jax.experimental.pallas import tpu as pltpu
from jax.sharding import PartitionSpec as P

MESH = pl.DeviceIdType.MESH
NT = (((1,), (1,)), ((), ()))


def fit(function, count):
    nodes = 0.125 + 0.125 * np.cos(np.pi * (np.arange(64) + 0.5) / 64)
    series = np.polynomial.chebyshev.Chebyshev.fit(nodes, function(np.sqrt(nodes)), count - 1, domain=[0, 0.25])
    return [float(c) for c in series.convert(kind=np.polynomial.Polynomial).coef]


SIN_HALF = fit(lambda r: math.sqrt(2) * np.sin(np.pi * r) / r, 5)
COS_HALF = fit(lambda r: math.sqrt(2) * np.cos(np.pi * r), 5)


def horner(coefficients, y):
    total = coefficients[-1]
    for c in coefficients[-2::-1]:
        total = total * y + c
    return total


def fraction(turns):
    return turns - ((turns + 12582912.0) - 12582912.0)


def cos_turns(turns):
    r = fraction(turns)
    s = r * horner(SIN_HALF, r * r)
    return 1.0 - s * s


def cos_sin_turns(turns):
    r = fraction(turns)
    y = r * r
    s = r * horner(SIN_HALF, y)
    return 1.0 - s * s, s * horner(COS_HALF, y)


def kernel(dims, bins, samples, delays, out, table, held, delay, quarter, other_delay, spec, gath, steer, acc,
           power_out, power_in, sample_sem, delay_sem, send_sem, fwd_sem, recv_sem, quarter_send, quarter_recv,
           power_sem):
    T, Z, Y, bin_count, nb, wb, rows, chunk_segs, parts, group, steps, slots = dims
    mics_here, length = samples.shape[1], samples.shape[2]
    points, mics = delays.shape
    seg_groups = steps // parts
    t, m = lax.axis_index("tm"), lax.axis_index("mic")
    z, y = lax.div(m, Y), lax.rem(m, Y)
    side = lax.rem(z, 2)

    def mic_of(z2, y2):
        return z2 * Y + y2

    def fetch(i, slot):
        c, q = lax.div(i, parts), lax.rem(i, parts)
        return pltpu.make_async_copy(
            samples.at[pl.ds(c * chunk_segs, chunk_segs), pl.ds(pl.multiple_of(q * group, group), group)],
            held.at[slot], sample_sem.at[slot])

    pltpu.make_async_copy(delays, delay, delay_sem).start()
    for i in range(min(slots, steps)):
        fetch(i, i).start()

    near = [(lax.rem(t + a, T), lax.rem(z + k, Z), y) for k in range(Z) for a in range(T) if k or a]
    across = [(lax.rem(t + a, T), z, 1 - y) for a in range(T)]
    peers = near + across
    partner = mic_of(z + 1 - 2 * side, y)
    barrier = pltpu.get_barrier_semaphore()
    for t2, z2, y2 in peers:
        pl.semaphore_signal(barrier, inc=1, device_id={"tm": t2, "mic": mic_of(z2, y2)}, device_id_type=MESH)

    table_rows = 2 * bin_count
    row = lax.broadcasted_iota(jnp.int32, (table_rows, 128), 0)
    lane = lax.broadcasted_iota(jnp.int32, (table_rows, 128), 1)
    bin_of = (row // (2 * wb)) * wb + row % wb
    scale = jnp.zeros((table_rows, 128), jnp.float32)
    for i in range(bin_count):
        scale = jnp.where(bin_of == i, bins[i].astype(jnp.float32) * (1.0 / length), scale)
    shift = jnp.where((row // wb) % 2 == 1, jnp.float32(0.25), jnp.float32(0.0))
    lane8 = lax.broadcasted_iota(jnp.int32, (8, 128), 1)

    def window_at(j, like):
        return 0.5 - 0.5 * cos_turns((like + j * 128).astype(jnp.float32) * (1.0 / length))

    def norm_step(j, total):
        w = window_at(j, lane8)
        return total + w * w

    norm = jnp.sum(lax.fori_loop(0, length // 128, norm_step, jnp.zeros((8, 128), jnp.float32), unroll=4),
                   axis=1, keepdims=True)[0:1]
    inverse = 1.0 / jnp.sqrt(norm)

    def table_step(j, carry):
        w = window_at(j, lane8)[0:1] * inverse
        turns = (lane + j * 128).astype(jnp.float32) * scale + shift
        table[:, pl.ds(pl.multiple_of(j * 128, 128), 128)] = (w * cos_turns(turns)).astype(jnp.bfloat16)
        return carry

    lax.fori_loop(0, length // 128, table_step, 0, unroll=4)

    own_scale = [bins[t * nb + side * wb + b].astype(jnp.float32) * (1.0 / length) for b in range(wb)]
    width = 512 if mics % 512 == 0 else 128
    share = points // T

    def block_of(i, m2):
        g, q = lax.div(i, parts), lax.rem(i, parts)
        return gath.at[m2, pl.ds(pl.multiple_of(g * T * rows, T * rows), T * rows),
                       pl.ds(pl.multiple_of(q * group, group), group)]

    def slot_of(i):
        g, q = lax.div(i, parts), lax.rem(i, parts)
        return gath.at[m, pl.ds(pl.multiple_of(g * T * rows + t * rows, rows), rows),
                       pl.ds(pl.multiple_of(q * group, group), group)]

    def source_of(i, t2, z2):
        worker = t2 * 2 + lax.rem(z2, 2)
        return spec.at[i, pl.ds(pl.multiple_of(worker * rows, rows), rows)]

    def push(i, index, t2, z2, y2):
        return pltpu.make_async_remote_copy(
            src_ref=source_of(i, t2, z2), dst_ref=slot_of(i),
            send_sem=send_sem.at[i, index], recv_sem=recv_sem.at[i, m],
            device_id={"tm": t2, "mic": mic_of(z2, y2)}, device_id_type=MESH)

    def forward(i, k):
        m2 = mic_of(lax.rem(z + k, Z), y)
        return pltpu.make_async_remote_copy(
            src_ref=block_of(i, m2), dst_ref=block_of(i, m2),
            send_sem=fwd_sem.at[i, k - 1], recv_sem=recv_sem.at[i, m2],
            device_id={"tm": t, "mic": mic_of(z, 1 - y)}, device_id_type=MESH)

    def arrived(i, m2):
        pltpu.make_async_copy(block_of(i, m2), block_of(i, m2), recv_sem.at[i, m2]).wait()

    def send_chunk(i):
        for index, peer in enumerate(peers):
            push(i, index, *peer).start()
        pltpu.make_async_copy(source_of(i, t, z), slot_of(i), recv_sem.at[i, m]).start()

    def pass_on(i):
        for k in range(1, Z):
            arrived(i, mic_of(lax.rem(z + k, Z), y))
            forward(i, k).start()

    def share_of(t2):
        return other_delay.at[pl.ds(pl.multiple_of(t2 * share, share), share)]

    def give_share():
        return pltpu.make_async_remote_copy(
            src_ref=quarter, dst_ref=share_of(t), send_sem=quarter_send.at[0], recv_sem=quarter_recv.at[t],
            device_id={"tm": t, "mic": partner}, device_id_type=MESH)

    def share_on(a):
        return pltpu.make_async_remote_copy(
            src_ref=share_of(t), dst_ref=share_of(t), send_sem=quarter_send.at[a], recv_sem=quarter_recv.at[t],
            device_id={"tm": lax.rem(t + a, T), "mic": m}, device_id_type=MESH)

    def share_arrived(t2):
        pltpu.make_async_copy(share_of(t2), share_of(t2), quarter_recv.at[t2]).wait()

    pltpu.make_async_copy(delays, delay, delay_sem).wait()
    quarter[...] = delay[pl.ds(pl.multiple_of(t * share, share), share), :].astype(jnp.int16)
    pl.semaphore_wait(barrier, len(peers))
    give_share().start()

    def step(i, carry):
        slot = lax.rem(i, slots)
        fetch(i, slot).wait()
        block = held[slot].reshape(chunk_segs * group, length)
        found = lax.dot_general(table[...], block, NT, preferred_element_type=jnp.float32)
        found = [found[:, s * group:(s + 1) * group] for s in range(chunk_segs)]
        for worker in range(2 * T):
            lines = [f[worker * 2 * wb:(worker + 1) * 2 * wb] for f in found]
            spec[i, worker * rows:(worker + 1) * rows, :] = jnp.concatenate(lines, axis=0).astype(jnp.bfloat16)

        @pl.when(i + slots < steps)
        def _():
            fetch(i + slots, slot).start()

        send_chunk(i)

        @pl.when(i == 1)
        def _():
            share_arrived(t)
            for a in range(1, T):
                share_on(a).start()

        @pl.when(i >= 2)
        def _():
            pass_on(i - 2)

        return carry

    lax.fori_loop(0, steps, step, 0)

    piece = 16
    pieces = points // piece
    turn_of = {pieces // 8: steps - 2, pieces // 2: steps - 1}

    def steer_step(half, i):
        first = pl.multiple_of(i * piece, piece)
        source = other_delay if half else delay
        for start in range(0, mics, width):
            turns = source[pl.ds(first, piece), start:start + width].astype(jnp.int32).astype(jnp.float32)
            for b in range(wb):
                cosine, sine = cos_sin_turns(turns * own_scale[b])
                steer[b, 0, half, pl.ds(first, piece), start:start + width] = cosine.astype(jnp.bfloat16)
                steer[b, 1, half, pl.ds(first, piece), start:start + width] = sine.astype(jnp.bfloat16)

    def own_step(i, carry):
        steer_step(0, i)
        for turn, late in turn_of.items():
            @pl.when(i == turn)
            def _():
                pass_on(late)

        return carry

    def partner_step(i, carry):
        steer_step(1, i)
        return carry

    lax.fori_loop(0, pieces, own_step, 0)
    for a in range(1, T):
        share_arrived(lax.rem(t + a, T))
    lax.fori_loop(0, pieces, partner_step, 0)

    acc[...] = jnp.zeros_like(acc)

    def add_block(m2):
        columns = pl.ds(pl.multiple_of(m2 * mics_here, mics_here), mics_here)
        lhs = steer[:, :, :, :, columns].reshape(wb * 4 * points, mics_here)
        acc[...] += lax.dot_general(lhs, gath[m2], NT, preferred_element_type=jnp.float32)

    def own_y(k, carry):
        m2 = mic_of(lax.rem(z + k, Z), y)

        @pl.when(k == 0)
        def _():
            for i in range(steps):
                arrived(i, m2)

        add_block(m2)
        return carry

    lax.fori_loop(0, Z, own_y, 0)

    def other_y(k, carry):
        m2 = mic_of(lax.rem(z + k, Z), 1 - y)
        for i in range(steps):
            arrived(i, m2)
        add_block(m2)
        return carry

    lax.fori_loop(0, Z, other_y, 0)

    columns = seg_groups * T * rows
    column = lax.broadcasted_iota(jnp.int32, (2 * points, columns), 1)
    own, theirs = [], []
    for b in range(wb):
        along_cos = acc[(4 * b) * points:(4 * b + 2) * points]
        along_sin = acc[(4 * b + 2) * points:(4 * b + 4) * points]
        real = along_cos - pltpu.roll(along_sin, columns - wb, axis=1)
        imag = pltpu.roll(along_cos, columns - wb, axis=1) + along_sin
        power = jnp.where(column % (2 * wb) == b, real * real + imag * imag, 0.0)
        total = jnp.sum(power.T, axis=0, keepdims=True) * (1.0 / (mics * seg_groups * chunk_segs * T))
        own.append(total[:, :points])
        theirs.append(total[:, points:])
    power_out[...] = jnp.zeros_like(power_out)
    power_out[0:wb, :] = jnp.concatenate(theirs, axis=0)
    swap = pltpu.make_async_remote_copy(
        src_ref=power_out, dst_ref=power_in, send_sem=power_sem.at[0], recv_sem=power_sem.at[1],
        device_id={"tm": t, "mic": partner}, device_id_type=MESH)
    swap.start()

    def drain(i, carry):
        for index, peer in enumerate(peers):
            push(i, index, *peer).wait_send()
        for k in range(1, Z):
            forward(i, k).wait_send()
        return carry

    lax.fori_loop(0, steps, drain, 0)
    give_share().wait_send()
    for a in range(1, T):
        share_on(a).wait_send()
    swap.wait()
    own = jnp.concatenate(own, axis=0)
    came = power_in[0:wb, :]
    out[0:wb, :] = jnp.where(side == 0, own, came)
    out[wb:2 * wb, :] = jnp.where(side == 0, came, own)


def per_device(T, M, samples, bin_ids, delays):
    segs, mics_here, length = samples.shape
    points, mics = delays.shape
    bin_count = bin_ids.shape[0]
    Y = 2
    Z = M // Y
    nb = bin_count // T
    wb = nb // 2
    chunk_segs = max(1, 16 // (2 * wb))
    rows = chunk_segs * 2 * wb
    group = min(mics_here, 256)
    parts = mics_here // group
    steps = segs // chunk_segs * parts
    slots = min(steps, 3)
    columns = segs // chunk_segs * T * rows
    peers = T * Z - 1 + T
    dims = (T, Z, Y, bin_count, nb, wb, rows, chunk_segs, parts, group, steps, slots)
    DMA = pltpu.SemaphoreType.DMA
    return pl.pallas_call(
        functools.partial(kernel, dims),
        out_shape=jax.ShapeDtypeStruct((nb, points), jnp.float32),
        in_specs=[
            pl.BlockSpec(memory_space=pltpu.SMEM),
            pl.BlockSpec(memory_space=pl.ANY),
            pl.BlockSpec(memory_space=pl.ANY),
        ],
        out_specs=pl.BlockSpec(memory_space=pltpu.VMEM),
        scratch_shapes=[
            pltpu.VMEM((2 * bin_count, length), jnp.bfloat16),
            pltpu.VMEM((slots, chunk_segs, group, length), jnp.bfloat16),
            pltpu.VMEM((points, mics), jnp.int32),
            pltpu.VMEM((points // T, mics), jnp.int16),
            pltpu.VMEM((points, mics), jnp.int16),
            pltpu.VMEM((steps, 2 * T * rows, group), jnp.bfloat16),
            pltpu.VMEM((M, columns, mics_here), jnp.bfloat16),
            pltpu.VMEM((wb, 2, 2, points, mics), jnp.bfloat16),
            pltpu.VMEM((wb * 4 * points, columns), jnp.float32),
            pltpu.VMEM((8, points), jnp.float32),
            pltpu.VMEM((8, points), jnp.float32),
            DMA((slots,)),
            DMA(()),
            DMA((steps, peers)),
            DMA((steps, Z - 1)),
            DMA((steps, M)),
            DMA((T,)),
            DMA((T,)),
            DMA((2,)),
        ],
        compiler_params=pltpu.CompilerParams(
            collective_id=0, has_side_effects=True, vmem_limit_bytes=56 * 1024 * 1024),
        cost_estimate=pl.CostEstimate(
            flops=2 * samples.size * 2 * bin_count, bytes_accessed=samples.size * 2, transcendentals=0),
    )(bin_ids, samples, delays)


def solution(mesh):
    placed = (P("tm", "mic", None), P(), P("mic", None))
    return jax.shard_map(
        functools.partial(per_device, mesh.shape["tm"], mesh.shape["mic"]),
        mesh=mesh, in_specs=placed, out_specs=P("tm", "mic"), check_vma=False)
```

```python
import functools
import math

import jax
import jax.numpy as jnp
import numpy as np
from jax import lax
from jax.experimental import pallas as pl
from jax.experimental.pallas import tpu as pltpu
from jax.sharding import PartitionSpec as P

MESH = pl.DeviceIdType.MESH
NT = (((1,), (1,)), ((), ()))


def fit(function, count):
    nodes = 0.125 + 0.125 * np.cos(np.pi * (np.arange(64) + 0.5) / 64)
    series = np.polynomial.chebyshev.Chebyshev.fit(nodes, function(np.sqrt(nodes)), count - 1, domain=[0, 0.25])
    return [float(c) for c in series.convert(kind=np.polynomial.Polynomial).coef]


SIN_HALF = fit(lambda r: math.sqrt(2) * np.sin(np.pi * r) / r, 5)
COS_HALF = fit(lambda r: math.sqrt(2) * np.cos(np.pi * r), 5)


def horner(coefficients, y):
    total = coefficients[-1]
    for c in coefficients[-2::-1]:
        total = total * y + c
    return total


def fraction(turns):
    return turns - ((turns + 12582912.0) - 12582912.0)


def cos_turns(turns):
    r = fraction(turns)
    s = r * horner(SIN_HALF, r * r)
    return 1.0 - s * s


def cos_sin_turns(turns):
    r = fraction(turns)
    y = r * r
    s = r * horner(SIN_HALF, y)
    return 1.0 - s * s, s * horner(COS_HALF, y)


def kernel(dims, bins, samples, delays, out, table, held, delay, quarter, other_delay, spec, gath, steer, acc,
           power_out, power_in, sample_sem, delay_sem, send_sem, fwd_sem, recv_sem, quarter_send, quarter_recv,
           power_sem):
    T, Z, Y, bin_count, nb, wb, rows, chunk_segs, parts, group, steps, slots = dims
    mics_here, length = samples.shape[1], samples.shape[2]
    points, mics = delays.shape
    seg_groups = steps // parts
    t, m = lax.axis_index("tm"), lax.axis_index("mic")
    z, y = lax.div(m, Y), lax.rem(m, Y)
    side = lax.rem(z, 2)

    def mic_of(z2, y2):
        return z2 * Y + y2

    def fetch(i, slot):
        c, q = lax.div(i, parts), lax.rem(i, parts)
        return pltpu.make_async_copy(
            samples.at[pl.ds(c * chunk_segs, chunk_segs), pl.ds(pl.multiple_of(q * group, group), group)],
            held.at[slot], sample_sem.at[slot])

    pltpu.make_async_copy(delays, delay, delay_sem).start()
    for i in range(min(slots, steps)):
        fetch(i, i).start()

    near = [(lax.rem(t + a, T), lax.rem(z + k, Z), y) for k in range(Z) for a in range(T) if k or a]
    across = [(lax.rem(t + a, T), z, 1 - y) for a in range(T)]
    peers = near + across
    partner = mic_of(z + 1 - 2 * side, y)
    barrier = pltpu.get_barrier_semaphore()
    for t2, z2, y2 in peers:
        pl.semaphore_signal(barrier, inc=1, device_id={"tm": t2, "mic": mic_of(z2, y2)}, device_id_type=MESH)

    table_rows = 2 * bin_count
    row = lax.broadcasted_iota(jnp.int32, (table_rows, 128), 0)
    lane = lax.broadcasted_iota(jnp.int32, (table_rows, 128), 1)
    bin_of = (row // (2 * wb)) * wb + row % wb
    scale = jnp.zeros((table_rows, 128), jnp.float32)
    for i in range(bin_count):
        scale = jnp.where(bin_of == i, bins[i].astype(jnp.float32) * (1.0 / length), scale)
    shift = jnp.where((row // wb) % 2 == 1, jnp.float32(0.25), jnp.float32(0.0))
    lane8 = lax.broadcasted_iota(jnp.int32, (8, 128), 1)

    def window_at(j, like):
        return 0.5 - 0.5 * cos_turns((like + j * 128).astype(jnp.float32) * (1.0 / length))

    def norm_step(j, total):
        w = window_at(j, lane8)
        return total + w * w

    norm = jnp.sum(lax.fori_loop(0, length // 128, norm_step, jnp.zeros((8, 128), jnp.float32), unroll=4),
                   axis=1, keepdims=True)[0:1]
    inverse = 1.0 / jnp.sqrt(norm)

    def table_step(j, carry):
        w = window_at(j, lane8)[0:1] * inverse
        turns = (lane + j * 128).astype(jnp.float32) * scale + shift
        table[:, pl.ds(pl.multiple_of(j * 128, 128), 128)] = (w * cos_turns(turns)).astype(jnp.bfloat16)
        return carry

    lax.fori_loop(0, length // 128, table_step, 0, unroll=4)

    own_scale = [bins[t * nb + side * wb + b].astype(jnp.float32) * (1.0 / length) for b in range(wb)]
    width = 512 if mics % 512 == 0 else 128
    share = points // T

    def block_of(i, m2):
        g, q = lax.div(i, parts), lax.rem(i, parts)
        return gath.at[m2, pl.ds(pl.multiple_of(g * T * rows, T * rows), T * rows),
                       pl.ds(pl.multiple_of(q * group, group), group)]

    def slot_of(i):
        g, q = lax.div(i, parts), lax.rem(i, parts)
        return gath.at[m, pl.ds(pl.multiple_of(g * T * rows + t * rows, rows), rows),
                       pl.ds(pl.multiple_of(q * group, group), group)]

    def source_of(i, t2, z2):
        worker = t2 * 2 + lax.rem(z2, 2)
        return spec.at[i, pl.ds(pl.multiple_of(worker * rows, rows), rows)]

    def push(i, index, t2, z2, y2):
        return pltpu.make_async_remote_copy(
            src_ref=source_of(i, t2, z2), dst_ref=slot_of(i),
            send_sem=send_sem.at[i, index], recv_sem=recv_sem.at[i, m],
            device_id={"tm": t2, "mic": mic_of(z2, y2)}, device_id_type=MESH)

    def forward(i, k):
        m2 = mic_of(lax.rem(z + k, Z), y)
        return pltpu.make_async_remote_copy(
            src_ref=block_of(i, m2), dst_ref=block_of(i, m2),
            send_sem=fwd_sem.at[i, k - 1], recv_sem=recv_sem.at[i, m2],
            device_id={"tm": t, "mic": mic_of(z, 1 - y)}, device_id_type=MESH)

    def arrived(i, m2):
        pltpu.make_async_copy(block_of(i, m2), block_of(i, m2), recv_sem.at[i, m2]).wait()

    def send_chunk(i):
        for index, peer in enumerate(peers):
            push(i, index, *peer).start()
        pltpu.make_async_copy(source_of(i, t, z), slot_of(i), recv_sem.at[i, m]).start()

    def pass_on(i):
        for k in range(1, Z):
            arrived(i, mic_of(lax.rem(z + k, Z), y))
            forward(i, k).start()

    def share_of(t2):
        return other_delay.at[pl.ds(pl.multiple_of(t2 * share, share), share)]

    def give_share():
        return pltpu.make_async_remote_copy(
            src_ref=quarter, dst_ref=share_of(t), send_sem=quarter_send.at[0], recv_sem=quarter_recv.at[t],
            device_id={"tm": t, "mic": partner}, device_id_type=MESH)

    beside = t + 1 - 2 * lax.rem(t, 2)
    over = lax.rem(t + T // 2, T)
    over_beside = lax.rem(beside + T // 2, T)

    def share_on(a):
        owner, target = ((t, beside), (t, over), (over, beside))[a - 1]
        return pltpu.make_async_remote_copy(
            src_ref=share_of(owner), dst_ref=share_of(owner), send_sem=quarter_send.at[a],
            recv_sem=quarter_recv.at[owner], device_id={"tm": target, "mic": m}, device_id_type=MESH)

    def share_arrived(t2):
        pltpu.make_async_copy(share_of(t2), share_of(t2), quarter_recv.at[t2]).wait()

    pltpu.make_async_copy(delays, delay, delay_sem).wait()
    quarter[...] = delay[pl.ds(pl.multiple_of(t * share, share), share), :].astype(jnp.int16)
    pl.semaphore_wait(barrier, len(peers))
    give_share().start()

    def step(i, carry):
        slot = lax.rem(i, slots)
        fetch(i, slot).wait()
        block = held[slot].reshape(chunk_segs * group, length)
        found = lax.dot_general(table[...], block, NT, preferred_element_type=jnp.float32)
        found = [found[:, s * group:(s + 1) * group] for s in range(chunk_segs)]
        for worker in range(2 * T):
            lines = [f[worker * 2 * wb:(worker + 1) * 2 * wb] for f in found]
            spec[i, worker * rows:(worker + 1) * rows, :] = jnp.concatenate(lines, axis=0).astype(jnp.bfloat16)

        @pl.when(i + slots < steps)
        def _():
            fetch(i + slots, slot).start()

        send_chunk(i)

        @pl.when(i == 1)
        def _():
            share_arrived(t)
            share_on(2).start()
            share_on(1).start()

        @pl.when(i >= 2)
        def _():
            pass_on(i - 2)

        return carry

    lax.fori_loop(0, steps, step, 0)

    piece = 16
    pieces = points // piece
    turn_of = {pieces // 8: steps - 2, pieces // 2: steps - 1}

    def steer_step(half, i):
        first = pl.multiple_of(i * piece, piece)
        source = other_delay if half else delay
        for start in range(0, mics, width):
            turns = source[pl.ds(first, piece), start:start + width].astype(jnp.int32).astype(jnp.float32)
            for b in range(wb):
                cosine, sine = cos_sin_turns(turns * own_scale[b])
                steer[b, 0, half, pl.ds(first, piece), start:start + width] = cosine.astype(jnp.bfloat16)
                steer[b, 1, half, pl.ds(first, piece), start:start + width] = sine.astype(jnp.bfloat16)

    def own_step(i, carry):
        steer_step(0, i)

        @pl.when(i == pieces // 4)
        def _():
            share_arrived(over)
            share_on(3).start()

        for turn, late in turn_of.items():
            @pl.when(i == turn)
            def _():
                pass_on(late)

        return carry

    lax.fori_loop(0, pieces, own_step, 0)
    share_pieces = share // piece

    def partner_steps(owner):
        def one(n, carry):
            steer_step(1, owner * share_pieces + n)
            return carry

        lax.fori_loop(0, share_pieces, one, 0)

    partner_steps(t)
    share_arrived(beside)
    partner_steps(beside)
    partner_steps(over)
    share_arrived(over_beside)
    partner_steps(over_beside)

    acc[...] = jnp.zeros_like(acc)

    def add_block(m2):
        columns = pl.ds(pl.multiple_of(m2 * mics_here, mics_here), mics_here)
        lhs = steer[:, :, :, :, columns].reshape(wb * 4 * points, mics_here)
        acc[...] += lax.dot_general(lhs, gath[m2], NT, preferred_element_type=jnp.float32)

    def own_y(k, carry):
        m2 = mic_of(lax.rem(z + k, Z), y)

        @pl.when(k == 0)
        def _():
            for i in range(steps):
                arrived(i, m2)

        add_block(m2)
        return carry

    lax.fori_loop(0, Z, own_y, 0)

    def other_y(k, carry):
        m2 = mic_of(lax.rem(z + k, Z), 1 - y)
        for i in range(steps):
            arrived(i, m2)
        add_block(m2)
        return carry

    lax.fori_loop(0, Z, other_y, 0)

    columns = seg_groups * T * rows
    column = lax.broadcasted_iota(jnp.int32, (2 * points, columns), 1)
    own, theirs = [], []
    for b in range(wb):
        along_cos = acc[(4 * b) * points:(4 * b + 2) * points]
        along_sin = acc[(4 * b + 2) * points:(4 * b + 4) * points]
        real = along_cos - pltpu.roll(along_sin, columns - wb, axis=1)
        imag = pltpu.roll(along_cos, columns - wb, axis=1) + along_sin
        power = jnp.where(column % (2 * wb) == b, real * real + imag * imag, 0.0)
        total = jnp.sum(power.T, axis=0, keepdims=True) * (1.0 / (mics * seg_groups * chunk_segs * T))
        own.append(total[:, :points])
        theirs.append(total[:, points:])
    power_out[...] = jnp.zeros_like(power_out)
    power_out[0:wb, :] = jnp.concatenate(theirs, axis=0)
    swap = pltpu.make_async_remote_copy(
        src_ref=power_out, dst_ref=power_in, send_sem=power_sem.at[0], recv_sem=power_sem.at[1],
        device_id={"tm": t, "mic": partner}, device_id_type=MESH)
    swap.start()

    def drain(i, carry):
        for index, peer in enumerate(peers):
            push(i, index, *peer).wait_send()
        for k in range(1, Z):
            forward(i, k).wait_send()
        return carry

    lax.fori_loop(0, steps, drain, 0)
    give_share().wait_send()
    for a in range(1, 4):
        share_on(a).wait_send()
    swap.wait()
    own = jnp.concatenate(own, axis=0)
    came = power_in[0:wb, :]
    out[0:wb, :] = jnp.where(side == 0, own, came)
    out[wb:2 * wb, :] = jnp.where(side == 0, came, own)


def per_device(T, M, samples, bin_ids, delays):
    segs, mics_here, length = samples.shape
    points, mics = delays.shape
    bin_count = bin_ids.shape[0]
    Y = 2
    Z = M // Y
    nb = bin_count // T
    wb = nb // 2
    chunk_segs = max(1, 16 // (2 * wb))
    rows = chunk_segs * 2 * wb
    group = min(mics_here, 256)
    parts = mics_here // group
    steps = segs // chunk_segs * parts
    slots = min(steps, 3)
    columns = segs // chunk_segs * T * rows
    peers = T * Z - 1 + T
    dims = (T, Z, Y, bin_count, nb, wb, rows, chunk_segs, parts, group, steps, slots)
    DMA = pltpu.SemaphoreType.DMA
    return pl.pallas_call(
        functools.partial(kernel, dims),
        out_shape=jax.ShapeDtypeStruct((nb, points), jnp.float32),
        in_specs=[
            pl.BlockSpec(memory_space=pltpu.SMEM),
            pl.BlockSpec(memory_space=pl.ANY),
            pl.BlockSpec(memory_space=pl.ANY),
        ],
        out_specs=pl.BlockSpec(memory_space=pltpu.VMEM),
        scratch_shapes=[
            pltpu.VMEM((2 * bin_count, length), jnp.bfloat16),
            pltpu.VMEM((slots, chunk_segs, group, length), jnp.bfloat16),
            pltpu.VMEM((points, mics), jnp.int32),
            pltpu.VMEM((points // T, mics), jnp.int16),
            pltpu.VMEM((points, mics), jnp.int16),
            pltpu.VMEM((steps, 2 * T * rows, group), jnp.bfloat16),
            pltpu.VMEM((M, columns, mics_here), jnp.bfloat16),
            pltpu.VMEM((wb, 2, 2, points, mics), jnp.bfloat16),
            pltpu.VMEM((wb * 4 * points, columns), jnp.float32),
            pltpu.VMEM((8, points), jnp.float32),
            pltpu.VMEM((8, points), jnp.float32),
            DMA((slots,)),
            DMA(()),
            DMA((steps, peers)),
            DMA((steps, Z - 1)),
            DMA((steps, M)),
            DMA((4,)),
            DMA((T,)),
            DMA((2,)),
        ],
        compiler_params=pltpu.CompilerParams(
            collective_id=0, has_side_effects=True, vmem_limit_bytes=56 * 1024 * 1024),
        cost_estimate=pl.CostEstimate(
            flops=2 * samples.size * 2 * bin_count, bytes_accessed=samples.size * 2, transcendentals=0),
    )(bin_ids, samples, delays)


def solution(mesh):
    placed = (P("tm", "mic", None), P(), P("mic", None))
    return jax.shard_map(
        functools.partial(per_device, mesh.shape["tm"], mesh.shape["mic"]),
        mesh=mesh, in_specs=placed, out_specs=P("tm", "mic"), check_vma=False)
```
